32 devices in a mesh: face: 4 (over z), tile: 8 (over y, x, core).
Axes of the slice: x: 2, y: 2, z: 4, core: 2. Of those that a mesh axis runs over, the one named last changes fastest.
Arguments:
- tracers: float32 [16, 32, 16, 1280], P('face', 'tile'), may hold values from -6 to 6
- basis_weights: float32 [2, 16, 32, 16, 16], P(None, 'face', 'tile'), may hold values from -1 to 1
- up_owner: int32 [2, 16, 32], P(None, 'face', 'tile'), may hold values from 0 to 4, as said below
- up_slot: int32 [2, 16, 32], P(None, 'face', 'tile'), may hold values from 0 to 15, as said below
- send_list: int32 [2, 16, 32], replicated, may hold values from 0 to 15, as said below
Outputs:
- transported: float32 [16, 32, 16, 1280], P('face', 'tile')
The draws below stay inside these ranges and needn't reach their ends.
Inputs may be any that keep to these rules, and one draw needn't show every extreme that they name: `up_owner`: 0: the upstream element is on the same device; 1 and 2: on the device before or after along face, cyclically; 3 and 4: before or after along tile. On one device in one step, each position of each neighbour's list toward it is named by at most one target element, and a device names positions 0 to k - 1 of a list, k between 1 and 4, with 4 reached in every draw. `up_slot`: below 4 where up_owner is not 0. `send_list`: entry [s, 4 f + j, 4 t + c] is the c-th local element that device (f, t) lists in step s for direction j (j = 0: toward face + 1, 1: toward face - 1, 2: toward tile + 1, 3: toward tile - 1); the entries of one list are distinct.
All inputs are finite; a program needn't handle non-finite values.
Results may differ from the reference program's by a relative error of at most 0.0001.
Values sent between devices are 32-bit elements; how exact they have to be, the bound alone decides.
A program may use at most 64 MiB of HBM per device.

```python
import jax
import jax.numpy as jnp
from jax import lax

TRACERS = 10
LEVELS = 128
NODES = 16
EDGE = 4
STEPS = 2
CAP = 4
NEX = 16
NEY = 32
N_FACE = 4
N_TILE = 8


def lagrange_rows(points):
    gll_nodes = [-1.0, -0.4472135955, 0.4472135955, 1.0]
    columns = []
    for first in range(4):
        term = jnp.ones_like(points)
        for other in range(4):
            if other != first:
                term = term * (points - gll_nodes[other]) / (gll_nodes[first] - gll_nodes[other])
        columns.append(term)
    return jnp.stack(columns, axis=-1)


def draw_basis_weights(key, part):
    key_x, key_y = jax.random.split(jax.random.fold_in(key, 11))
    shape = (STEPS, NEX, NEY, 16)
    points_x = jax.random.uniform(key_x, shape, jnp.float32, -1.0, 1.0)
    points_y = jax.random.uniform(key_y, shape, jnp.float32, -1.0, 1.0)
    basis_x = lagrange_rows(points_x)
    basis_y = lagrange_rows(points_y)
    product = basis_x[..., :, None] * basis_y[..., None, :]
    return product.reshape(STEPS, NEX, NEY, 16, 16).astype(jnp.float32)


def draw_routes(key):
    base = jax.random.fold_in(key, 7)
    key_count, key_order, key_own = jax.random.split(base, 3)
    elem_count = EDGE * EDGE
    counts = jax.random.randint(key_count, (STEPS, N_FACE, N_TILE, 4), 1, CAP + 1).astype(jnp.int32)
    counts = counts.at[:, 0, 0, 0].set(CAP)
    counts = counts.at[:, 0, 1, 0].set(max(CAP - 1, 1))
    scores = jax.random.randint(key_order, (STEPS, N_FACE, N_TILE, elem_count), 0, 1 << 20) * elem_count
    scores = scores + jnp.arange(elem_count, dtype=jnp.int32)
    order = jnp.argsort(scores, axis=-1)
    ranks = jnp.argsort(order, axis=-1).astype(jnp.int32)
    ends = jnp.cumsum(counts, axis=-1).astype(jnp.int32)
    starts = ends - counts
    passed = jnp.sum((ranks[..., None] >= ends[..., None, :]).astype(jnp.int32), axis=-1)
    remote = ranks < ends[..., 3:4]
    owners = jnp.where(remote, passed + 1, 0).astype(jnp.int32)
    start_of = jnp.take_along_axis(starts, jnp.minimum(passed, 3), axis=-1)
    own_slot = jax.random.randint(key_own, (STEPS, N_FACE, N_TILE, elem_count), 0, elem_count)
    own_slot = jnp.where(ranks == ends[..., 3:4], elem_count - 1, own_slot)
    slots = jnp.where(remote, ranks - start_of, own_slot).astype(jnp.int32)

    def layout(values):
        values = values.reshape(STEPS, N_FACE, N_TILE, EDGE, EDGE).transpose(0, 1, 3, 2, 4)
        return values.reshape(STEPS, NEX, NEY)
    return (layout(owners), layout(slots))


def draw_up_owner(key, part):
    return draw_routes(key)[0]


def draw_up_slot(key, part):
    return draw_routes(key)[1]


def draw_send_list(key, part):
    elem_count = EDGE * EDGE
    scores = jax.random.randint(jax.random.fold_in(key, 3), (STEPS, N_FACE, 4, N_TILE, elem_count), 0, 1 << 20)
    scores = scores * elem_count + jnp.arange(elem_count, dtype=jnp.int32)
    order = jnp.argsort(scores, axis=-1)[..., :CAP].astype(jnp.int32)
    return order.reshape(STEPS, 4 * N_FACE, N_TILE * CAP)


def block_levels(rng, dims, cuts, least, top_value):
    level, own = 1.0, jax.random.fold_in(rng, 6)
    for position, shards_of in cuts:
        heights = jnp.exp(jax.random.uniform(jax.random.fold_in(own, position), (shards_of,), jnp.float32, least / len(cuts), top_value / len(cuts)))
        level = level * jnp.repeat(heights, dims[position] // shards_of).reshape([-1 if axis == position else 1 for axis in range(len(dims))])
    return level


def scatter_about(rng, shape, spread, bound, cuts=(), kind=jnp.bfloat16):
    loudness = block_levels(rng, shape, cuts, -0.22, 0.18) if cuts else 1.0
    drawn = jax.random.normal(rng, shape, jnp.float32) * spread * loudness
    return jnp.minimum(jnp.maximum(drawn, -bound), bound).astype(kind)


def setup_inputs(seed: int = 0) -> dict:
    arg_keys = jax.random.split(jax.random.key(seed), 6)
    return {
        "tracers": scatter_about(arg_keys[0], (NEX, NEY, NODES, TRACERS * LEVELS), 1.0, 6.0, ((0, 4), (1, 8)), jnp.float32),
        "basis_weights": draw_basis_weights(jax.random.fold_in(arg_keys[5], 71), 0),
        "up_owner": draw_up_owner(jax.random.fold_in(arg_keys[5], 71), 0),
        "up_slot": draw_up_slot(jax.random.fold_in(arg_keys[5], 71), 0),
        "send_list": draw_send_list(jax.random.fold_in(arg_keys[5], 71), 0),
    }


def average_edges(interpolated):
    elem_rows = interpolated.shape[0]
    elem_cols = interpolated.shape[1]
    columns = interpolated.shape[3]
    node_grid = interpolated.reshape(elem_rows, elem_cols, 4, 4, columns).transpose(0, 2, 1, 3, 4)
    node_grid = node_grid.reshape(4 * elem_rows, 4 * elem_cols, columns)
    row_pos = jnp.arange(4 * elem_rows, dtype=jnp.int32) % 4
    at_first = (row_pos == 0)[:, None, None]
    at_last = (row_pos == 3)[:, None, None]
    row_pass = jnp.where(at_first, 0.5 * (node_grid + jnp.roll(node_grid, 1, 0)),
                         jnp.where(at_last, 0.5 * (node_grid + jnp.roll(node_grid, -1, 0)), node_grid))
    col_pos = jnp.arange(4 * elem_cols, dtype=jnp.int32) % 4
    col_first = (col_pos == 0)[None, :, None]
    col_last = (col_pos == 3)[None, :, None]
    col_pass = jnp.where(col_first, 0.5 * (row_pass + jnp.roll(row_pass, 1, 1)),
                         jnp.where(col_last, 0.5 * (row_pass + jnp.roll(row_pass, -1, 1)), row_pass))
    col_pass = col_pass.reshape(elem_rows, 4, elem_cols, 4, columns).transpose(0, 2, 1, 3, 4)
    return col_pass.reshape(elem_rows, elem_cols, 16, columns)


def reference(tracers, basis_weights, up_owner, up_slot, send_list):
    device_face = (jnp.arange(NEX, dtype=jnp.int32) // EDGE)[:, None]
    device_tile = (jnp.arange(NEY, dtype=jnp.int32) // EDGE)[None, :]
    tracer_field = tracers
    for sweep_index in range(STEPS):
        owners = up_owner[sweep_index]
        slot_index = up_slot[sweep_index]
        owner_face = jnp.where(owners == 1, (device_face - 1) % N_FACE,
                               jnp.where(owners == 2, (device_face + 1) % N_FACE, device_face))
        owner_tile = jnp.where(owners == 3, (device_tile - 1) % N_TILE,
                               jnp.where(owners == 4, (device_tile + 1) % N_TILE, device_tile))
        owner_face = owner_face.astype(jnp.int32)
        owner_tile = owner_tile.astype(jnp.int32)
        listed = send_list[sweep_index][owner_face * 4 + jnp.maximum(owners - 1, 0),
                                        owner_tile * CAP + jnp.minimum(slot_index, CAP - 1)]
        local_elem = jnp.where(owners == 0, slot_index, listed).astype(jnp.int32)
        source = tracer_field[owner_face * EDGE + local_elem // EDGE, owner_tile * EDGE + local_elem % EDGE]
        interpolated = jnp.einsum("xyij,xyjc->xyic", basis_weights[sweep_index], source,
                                  precision=lax.Precision.HIGHEST)
        interpolated = jnp.clip(interpolated, jnp.min(source, axis=2, keepdims=True),
                                jnp.max(source, axis=2, keepdims=True))
        tracer_field = average_edges(interpolated)
    return tracer_field
```

```python
import functools

import jax
import jax.numpy as jnp
from jax import lax
from jax.experimental import pallas as pl
from jax.experimental.pallas import tpu as pltpu
from jax.sharding import PartitionSpec as P

MESH = pl.DeviceIdType.MESH
NODES = 16
HIGHEST = lax.Precision.HIGHEST


def chunk_width(columns):
    for width in (256, 128):
        if columns % width == 0:
            return width
    return columns


def kernel(dims, tracers, weights, owners, slots, lists, out, *scratch):
    steps, side, cap, chunks, width = dims
    elems = side * side
    rows = elems * NODES
    count = steps * chunks
    received = scratch[:count]
    fields = scratch[count : count + chunks]
    (sending, mixing, source, moved, tile_out, tile_in, face_out, face_in,
     list_send, list_recv, tile_send, tile_recv, face_send, face_recv) = scratch[count + chunks :]

    face, tile = lax.axis_index("face"), lax.axis_index("tile")
    n_face, n_tile = lax.axis_size("face"), lax.axis_size("tile")
    south = (lax.rem(face + 1, n_face), tile)
    north = (lax.rem(face + n_face - 1, n_face), tile)
    east = (face, lax.rem(tile + 1, n_tile))
    west = (face, lax.rem(tile + n_tile - 1, n_tile))
    toward = (south, north, east, west)

    barrier = pltpu.get_barrier_semaphore()
    for device in toward:
        pl.semaphore_signal(barrier, inc=1, device_id=device, device_id_type=MESH)
    pl.semaphore_wait(barrier, 4)

    def list_copy(s, c, j):
        return pltpu.make_async_remote_copy(
            src_ref=sending.at[s, c, j],
            dst_ref=received[s * chunks + c].at[j],
            send_sem=list_send.at[s, c, j],
            recv_sem=list_recv.at[s, c, j],
            device_id=toward[j],
            device_id_type=MESH,
        )

    def edge_copy(s, c, j):
        store, land, send, recv = (
            (tile_out, tile_in, tile_send, tile_recv)
            if j >= 2
            else (face_out, face_in, face_send, face_recv)
        )
        return pltpu.make_async_remote_copy(
            src_ref=store.at[s, c, j % 2],
            dst_ref=land.at[s, c, j % 2],
            send_sem=send.at[s, c, j % 2],
            recv_sem=recv.at[s, c, j % 2],
            device_id=toward[j],
            device_id_type=MESH,
        )

    def columns(c):
        return slice(c * width, (c + 1) * width)

    def field_block(s, c, elem):
        if s == 0:
            return tracers[elem, :, columns(c)]
        return fields[c][elem]

    def send_lists(s, c):
        for j in range(4):
            def pick(k, carry, j=j):
                elem = lists[s, 4 * face + j, tile * cap + k]
                sending[s, c, j, k] = field_block(s, c, elem)
                return carry
            lax.fori_loop(0, cap, pick, 0, unroll=True)
            list_copy(s, c, j).start()

    for c in range(chunks):
        send_lists(0, c)

    lane = lax.broadcasted_iota(jnp.int32, (NODES, rows), 1)
    spread = jnp.where(
        (lane & (NODES - 1)) == lax.broadcasted_iota(jnp.int32, (NODES, rows), 0), 1.0, 0.0
    ).astype(jnp.float32)
    same = (lax.broadcasted_iota(jnp.int32, (rows, rows), 0) // NODES) == (
        lax.broadcasted_iota(jnp.int32, (rows, rows), 1) // NODES
    )
    for s in range(steps):
        repeated = jnp.dot(
            weights[s], spread, precision=HIGHEST, preferred_element_type=jnp.float32
        )
        mixing[s] = jnp.where(same, repeated, 0.0)

    node = lax.broadcasted_iota(jnp.int32, (NODES, width), 0)
    flat_node = lax.broadcasted_iota(jnp.int32, (rows, width), 0) & (NODES - 1)

    def shift(block, amount):
        amount = amount % block.shape[0]
        return pltpu.roll(block, amount, 0) if amount else block

    def grid_of(flat):
        return flat.reshape(side, side, NODES, width)

    def pack(blocks, shifts, place):
        packed = shift(blocks[0], shifts[0])
        for k in range(1, side):
            packed = jnp.where(place == k, shift(blocks[k], shifts[k]), packed)
        return packed

    def interpolate(s, c):
        for j in range(4):
            list_copy(s, c, j).wait_recv()
        arrived = received[s * chunks + c]

        def pick(elem, carry):
            owner = owners[s, elem // side, elem % side]
            slot = slots[s, elem // side, elem % side]
            own = field_block(s, c, slot)
            other = arrived[jnp.maximum(owner - 1, 0), jnp.minimum(slot, cap - 1)]
            source[elem] = jnp.where(owner == 0, own, other)
            return carry

        lax.fori_loop(0, elems, pick, 0, unroll=True)
        blocks = source[...]
        mixed = jnp.dot(
            mixing[s],
            blocks.reshape(rows, width),
            precision=HIGHEST,
            preferred_element_type=jnp.float32,
        ).reshape(elems, NODES, width)
        mixed = jnp.clip(
            mixed, jnp.min(blocks, axis=1, keepdims=True), jnp.max(blocks, axis=1, keepdims=True)
        )
        moved[c] = mixed
        grid = mixed.reshape(side, side, NODES, width)
        place = node & 3
        tile_out[s, c, 0] = pack(
            [grid[x, side - 1] for x in range(side)], [x - 3 for x in range(side)], place
        )
        tile_out[s, c, 1] = pack([grid[x, 0] for x in range(side)], list(range(side)), place)
        edge_copy(s, c, 2).start()
        edge_copy(s, c, 3).start()

    def average(flat, before, after, low, high, hop):
        return jnp.where(
            low,
            0.5 * (flat + shift(before, -hop)),
            jnp.where(high, 0.5 * (flat + shift(after, hop)), flat),
        )

    def average_columns(s, c):
        edge_copy(s, c, 2).wait_recv()
        edge_copy(s, c, 3).wait_recv()
        flat = moved[c].reshape(rows, width)
        grid = grid_of(flat)
        from_west, from_east = tile_in[s, c, 0], tile_in[s, c, 1]
        left = jnp.stack([shift(from_west, 3 - x) for x in range(side)])[:, None]
        right = jnp.stack([shift(from_east, -x) for x in range(side)])[:, None]
        before = jnp.concatenate([left, grid[:, : side - 1]], axis=1).reshape(rows, width)
        after = jnp.concatenate([grid[:, 1:], right], axis=1).reshape(rows, width)
        flat = average(flat, before, after, (flat_node & 3) == 0, (flat_node & 3) == 3, 3)
        moved[c] = flat.reshape(elems, NODES, width)
        grid = grid_of(flat)
        place = node >> 2
        face_out[s, c, 0] = pack(
            [grid[side - 1, y] for y in range(side)], [4 * y - 12 for y in range(side)], place
        )
        face_out[s, c, 1] = pack(
            [grid[0, y] for y in range(side)], [4 * y for y in range(side)], place
        )
        edge_copy(s, c, 0).start()
        edge_copy(s, c, 1).start()

    def average_rows(s, c):
        edge_copy(s, c, 0).wait_recv()
        edge_copy(s, c, 1).wait_recv()
        flat = moved[c].reshape(rows, width)
        grid = grid_of(flat)
        from_north, from_south = face_in[s, c, 0], face_in[s, c, 1]
        above = jnp.stack([shift(from_north, 12 - 4 * y) for y in range(side)])[None]
        below = jnp.stack([shift(from_south, -4 * y) for y in range(side)])[None]
        before = jnp.concatenate([above, grid[: side - 1]], axis=0).reshape(rows, width)
        after = jnp.concatenate([grid[1:], below], axis=0).reshape(rows, width)
        flat = average(flat, before, after, flat_node < 4, flat_node >= 12, 12)
        if s < steps - 1:
            fields[c][...] = flat.reshape(elems, NODES, width)
            send_lists(s + 1, c)
        else:
            out[:, :, columns(c)] = flat.reshape(elems, NODES, width)

    phases = (interpolate, average_columns, average_rows)
    for s in range(steps):
        for turn in range(chunks + 2):
            for phase in (2, 1, 0):
                c = turn - phase
                if 0 <= c < chunks:
                    phases[phase](s, c)

    for s in range(steps):
        for c in range(chunks):
            for j in range(4):
                list_copy(s, c, j).wait_send()
                edge_copy(s, c, j).wait_send()


def local(tracers, basis_weights, up_owner, up_slot, send_list):
    side = tracers.shape[0]
    columns = tracers.shape[3]
    steps = basis_weights.shape[0]
    elems = side * side
    rows = elems * NODES
    cap = send_list.shape[2] // lax.axis_size("tile")
    width = chunk_width(columns)
    chunks = columns // width
    dims = (steps, side, cap, chunks, width)
    vmem = pl.BlockSpec(memory_space=pltpu.VMEM)
    smem = pl.BlockSpec(memory_space=pltpu.SMEM)
    f32 = jnp.float32
    edges = pltpu.VMEM((steps, chunks, 2, NODES, width), f32)
    list_sems = pltpu.SemaphoreType.DMA((steps, chunks, 4))
    edge_sems = pltpu.SemaphoreType.DMA((steps, chunks, 2))
    result = pl.pallas_call(
        functools.partial(kernel, dims),
        out_shape=jax.ShapeDtypeStruct((elems, NODES, columns), f32),
        in_specs=[vmem, vmem, smem, smem, smem],
        out_specs=vmem,
        scratch_shapes=[pltpu.VMEM((4, cap, NODES, width), f32)] * (steps * chunks)
        + [pltpu.VMEM((elems, NODES, width), f32)] * chunks
        + [
            pltpu.VMEM((steps, chunks, 4, cap, NODES, width), f32),
            pltpu.VMEM((steps, rows, rows), f32),
            pltpu.VMEM((elems, NODES, width), f32),
            pltpu.VMEM((chunks, elems, NODES, width), f32),
            edges,
            edges,
            edges,
            edges,
            list_sems,
            list_sems,
            edge_sems,
            edge_sems,
            edge_sems,
            edge_sems,
        ],
        compiler_params=pltpu.CompilerParams(
            collective_id=0, has_side_effects=True, vmem_limit_bytes=40 * 1024 * 1024
        ),
        cost_estimate=pl.CostEstimate(
            flops=2 * steps * rows * NODES * columns,
            bytes_accessed=8 * rows * columns,
            transcendentals=0,
        ),
    )(
        tracers.reshape(elems, NODES, columns),
        basis_weights.reshape(steps, rows, NODES),
        up_owner,
        up_slot,
        send_list,
    )
    return result.reshape(side, side, NODES, columns)


def solution(mesh):
    return jax.shard_map(
        local,
        mesh=mesh,
        in_specs=(
            P("face", "tile", None, None),
            P(None, "face", "tile", None, None),
            P(None, "face", "tile"),
            P(None, "face", "tile"),
            P(),
        ),
        out_specs=P("face", "tile", None, None),
        check_vma=False,
    )
```

```python
import functools

import jax
import jax.numpy as jnp
from jax import lax
from jax.experimental import pallas as pl
from jax.experimental.pallas import tpu as pltpu
from jax.sharding import PartitionSpec as P

MESH = pl.DeviceIdType.MESH
NODES = 16
SLACK = 2
HIGHEST = lax.Precision.HIGHEST


def chunk_width(columns):
    for width in (256, 128):
        if columns % width == 0:
            return width
    return columns


def halves(values):
    high = values.astype(jnp.bfloat16)
    return high, (values - high.astype(jnp.float32)).astype(jnp.bfloat16)


def kernel(dims, *refs):
    steps, side, cap, chunks, width = dims
    elems = side * side
    rows = elems * NODES
    count = steps * chunks
    operands, out, scratch = refs[:5], refs[5], refs[6:]
    tracers, weights, owners, slots, lists, load_sems = scratch[:6]
    scratch = scratch[6:]
    loads = [
        pltpu.make_async_copy(operands[k], scratch_ref, load_sems.at[k])
        for k, scratch_ref in enumerate((tracers, weights, owners, slots, lists))
    ]
    for load in loads:
        load.start()
    received = scratch[:count]
    fields = scratch[count : count + chunks]
    (sending, mixing, source, moved, tile_out, tile_in, face_out, face_in,
     list_send, list_recv, tile_send, tile_recv, face_send, face_recv) = scratch[count + chunks :]

    face, tile = lax.axis_index("face"), lax.axis_index("tile")
    n_face, n_tile = lax.axis_size("face"), lax.axis_size("tile")
    south = (lax.rem(face + 1, n_face), tile)
    north = (lax.rem(face + n_face - 1, n_face), tile)
    east = (face, lax.rem(tile + 1, n_tile))
    west = (face, lax.rem(tile + n_tile - 1, n_tile))
    toward = (south, north, east, west)

    barrier = pltpu.get_barrier_semaphore()
    for device in toward:
        pl.semaphore_signal(barrier, inc=1, device_id=device, device_id_type=MESH)
    pl.semaphore_wait(barrier, 4)
    for load in loads:
        load.wait()

    def list_copy(s, c, j):
        return pltpu.make_async_remote_copy(
            src_ref=sending.at[s, c, j],
            dst_ref=received[s * chunks + c].at[j],
            send_sem=list_send.at[s, c, j],
            recv_sem=list_recv.at[s, c, j],
            device_id=toward[j],
            device_id_type=MESH,
        )

    def edge_copy(s, c, j):
        store, land, send, recv = (
            (tile_out, tile_in, tile_send, tile_recv)
            if j >= 2
            else (face_out, face_in, face_send, face_recv)
        )
        return pltpu.make_async_remote_copy(
            src_ref=store.at[s, c, j % 2],
            dst_ref=land.at[s, c, j % 2],
            send_sem=send.at[s, c, j % 2],
            recv_sem=recv.at[s, c, j % 2],
            device_id=toward[j],
            device_id_type=MESH,
        )

    def columns(c):
        return slice(c * width, (c + 1) * width)

    def field_block(s, c, elem):
        if s == 0:
            return tracers[elem, :, columns(c)]
        return fields[c][elem]

    def send_lists(s, c):
        for j in range(4):
            def pick(k, carry, j=j):
                elem = lists[s, 4 * face + j, tile * cap + k]
                sending[s, c, j, k] = field_block(s, c, elem)
                return carry
            lax.fori_loop(0, cap, pick, 0, unroll=True)
            list_copy(s, c, j).start()

    for c in range(chunks):
        send_lists(0, c)

    lane = lax.broadcasted_iota(jnp.int32, (NODES, rows), 1)
    spread = jnp.where(
        (lane & (NODES - 1)) == lax.broadcasted_iota(jnp.int32, (NODES, rows), 0), 1.0, 0.0
    ).astype(jnp.float32)
    same = (lax.broadcasted_iota(jnp.int32, (rows, rows), 0) // NODES) == (
        lax.broadcasted_iota(jnp.int32, (rows, rows), 1) // NODES
    )
    for s in range(steps):
        repeated = jnp.dot(
            weights[s], spread, precision=HIGHEST, preferred_element_type=jnp.float32
        )
        high, low = halves(jnp.where(same, repeated, 0.0))
        mixing[s] = jnp.concatenate([high, low, high], axis=1)

    node = lax.broadcasted_iota(jnp.int32, (NODES, width), 0)
    flat_node = lax.broadcasted_iota(jnp.int32, (rows, width), 0) & (NODES - 1)

    def shift(block, amount):
        amount = amount % block.shape[0]
        return pltpu.roll(block, amount, 0) if amount else block

    def grid_of(flat):
        return flat.reshape(side, side, NODES, width)

    def pack(blocks, shifts, place):
        packed = shift(blocks[0], shifts[0])
        for k in range(1, side):
            packed = jnp.where(place == k, shift(blocks[k], shifts[k]), packed)
        return packed

    def interpolate(s, c):
        for j in range(4):
            list_copy(s, c, j).wait_recv()
        arrived = received[s * chunks + c]

        def pick(elem, carry):
            owner = owners[s, elem // side, elem % side]
            slot = slots[s, elem // side, elem % side]
            own = field_block(s, c, slot)
            other = arrived[jnp.maximum(owner - 1, 0), jnp.minimum(slot, cap - 1)]
            source[elem] = jnp.where(owner == 0, own, other)
            return carry

        lax.fori_loop(0, elems, pick, 0, unroll=True)
        blocks = source[...]
        high, low = halves(blocks.reshape(rows, width))
        mixed = jnp.dot(
            mixing[s],
            jnp.concatenate([high, high, low], axis=0),
            preferred_element_type=jnp.float32,
        ).reshape(elems, NODES, width)
        mixed = jnp.clip(
            mixed, jnp.min(blocks, axis=1, keepdims=True), jnp.max(blocks, axis=1, keepdims=True)
        )
        moved[c] = mixed
        grid = mixed.reshape(side, side, NODES, width)
        place = node & 3
        tile_out[s, c, 0] = pack(
            [grid[x, side - 1] for x in range(side)], [x - 3 for x in range(side)], place
        )
        tile_out[s, c, 1] = pack([grid[x, 0] for x in range(side)], list(range(side)), place)
        edge_copy(s, c, 2).start()
        edge_copy(s, c, 3).start()

    def average(flat, before, after, low, high, hop):
        return jnp.where(
            low,
            0.5 * (flat + shift(before, -hop)),
            jnp.where(high, 0.5 * (flat + shift(after, hop)), flat),
        )

    def average_columns(s, c):
        edge_copy(s, c, 2).wait_recv()
        edge_copy(s, c, 3).wait_recv()
        flat = moved[c].reshape(rows, width)
        grid = grid_of(flat)
        from_west, from_east = tile_in[s, c, 0], tile_in[s, c, 1]
        left = jnp.stack([shift(from_west, 3 - x) for x in range(side)])[:, None]
        right = jnp.stack([shift(from_east, -x) for x in range(side)])[:, None]
        before = jnp.concatenate([left, grid[:, : side - 1]], axis=1).reshape(rows, width)
        after = jnp.concatenate([grid[:, 1:], right], axis=1).reshape(rows, width)
        flat = average(flat, before, after, (flat_node & 3) == 0, (flat_node & 3) == 3, 3)
        moved[c] = flat.reshape(elems, NODES, width)
        grid = grid_of(flat)
        place = node >> 2
        face_out[s, c, 0] = pack(
            [grid[side - 1, y] for y in range(side)], [4 * y - 12 for y in range(side)], place
        )
        face_out[s, c, 1] = pack(
            [grid[0, y] for y in range(side)], [4 * y for y in range(side)], place
        )
        edge_copy(s, c, 0).start()
        edge_copy(s, c, 1).start()

    def average_rows(s, c):
        edge_copy(s, c, 0).wait_recv()
        edge_copy(s, c, 1).wait_recv()
        flat = moved[c].reshape(rows, width)
        grid = grid_of(flat)
        from_north, from_south = face_in[s, c, 0], face_in[s, c, 1]
        above = jnp.stack([shift(from_north, 12 - 4 * y) for y in range(side)])[None]
        below = jnp.stack([shift(from_south, -4 * y) for y in range(side)])[None]
        before = jnp.concatenate([above, grid[: side - 1]], axis=0).reshape(rows, width)
        after = jnp.concatenate([grid[1:], below], axis=0).reshape(rows, width)
        flat = average(flat, before, after, flat_node < 4, flat_node >= 12, 12)
        if s < steps - 1:
            fields[c][...] = flat.reshape(elems, NODES, width)
            send_lists(s + 1, c)
        else:
            out[:, :, columns(c)] = flat.reshape(elems, NODES, width)

    phases = (interpolate, average_columns, average_rows)
    for s in range(steps):
        for turn in range(chunks + 2 * SLACK):
            for phase in (2, 1, 0):
                c = turn - SLACK * phase
                if 0 <= c < chunks:
                    phases[phase](s, c)

    for s in range(steps):
        for c in range(chunks):
            for j in range(4):
                list_copy(s, c, j).wait_send()
                edge_copy(s, c, j).wait_send()


def local(tracers, basis_weights, up_owner, up_slot, send_list):
    side = tracers.shape[0]
    columns = tracers.shape[3]
    steps = basis_weights.shape[0]
    elems = side * side
    rows = elems * NODES
    cap = send_list.shape[2] // lax.axis_size("tile")
    width = chunk_width(columns)
    chunks = columns // width
    dims = (steps, side, cap, chunks, width)
    vmem = pl.BlockSpec(memory_space=pltpu.VMEM)
    whole = pl.BlockSpec(memory_space=pl.ANY)
    f32 = jnp.float32
    edges = pltpu.VMEM((steps, chunks, 2, NODES, width), f32)
    list_sems = pltpu.SemaphoreType.DMA((steps, chunks, 4))
    edge_sems = pltpu.SemaphoreType.DMA((steps, chunks, 2))
    result = pl.pallas_call(
        functools.partial(kernel, dims),
        out_shape=jax.ShapeDtypeStruct((elems, NODES, columns), f32),
        in_specs=[whole] * 5,
        out_specs=vmem,
        scratch_shapes=[
            pltpu.VMEM((elems, NODES, columns), f32),
            pltpu.VMEM((steps, rows, NODES), f32),
            pltpu.SMEM(up_owner.shape, jnp.int32),
            pltpu.SMEM(up_slot.shape, jnp.int32),
            pltpu.SMEM(send_list.shape, jnp.int32),
            pltpu.SemaphoreType.DMA((5,)),
        ]
        + [pltpu.VMEM((4, cap, NODES, width), f32)] * (steps * chunks)
        + [pltpu.VMEM((elems, NODES, width), f32)] * chunks
        + [
            pltpu.VMEM((steps, chunks, 4, cap, NODES, width), f32),
            pltpu.VMEM((steps, rows, 3 * rows), jnp.bfloat16),
            pltpu.VMEM((elems, NODES, width), f32),
            pltpu.VMEM((chunks, elems, NODES, width), f32),
            edges,
            edges,
            edges,
            edges,
            list_sems,
            list_sems,
            edge_sems,
            edge_sems,
            edge_sems,
            edge_sems,
        ],
        compiler_params=pltpu.CompilerParams(
            collective_id=0, has_side_effects=True, vmem_limit_bytes=40 * 1024 * 1024
        ),
        cost_estimate=pl.CostEstimate(
            flops=2 * steps * rows * NODES * columns,
            bytes_accessed=8 * rows * columns,
            transcendentals=0,
        ),
    )(
        tracers.reshape(elems, NODES, columns),
        basis_weights.reshape(steps, rows, NODES),
        up_owner,
        up_slot,
        send_list,
    )
    return result.reshape(side, side, NODES, columns)


def solution(mesh):
    return jax.shard_map(
        local,
        mesh=mesh,
        in_specs=(
            P("face", "tile", None, None),
            P(None, "face", "tile", None, None),
            P(None, "face", "tile"),
            P(None, "face", "tile"),
            P(),
        ),
        out_specs=P("face", "tile", None, None),
        check_vma=False,
    )
```

```python
import functools

import jax
import jax.numpy as jnp
from jax import lax
from jax.experimental import pallas as pl
from jax.experimental.pallas import tpu as pltpu
from jax.sharding import PartitionSpec as P

MESH = pl.DeviceIdType.MESH
NODES = 16
SLACK = 2
AHEAD = 3
HIGHEST = lax.Precision.HIGHEST


def chunk_width(columns):
    for width in (256, 128):
        if columns % width == 0:
            return width
    return columns


def halves(values):
    high = values.astype(jnp.bfloat16)
    return high, (values - high.astype(jnp.float32)).astype(jnp.bfloat16)


def kernel(dims, *refs):
    steps, side, cap, chunks, width = dims
    elems = side * side
    rows = elems * NODES
    count = steps * chunks
    operands, out, scratch = refs[:5], refs[5], refs[6:]
    tracers, weights, owners, slots, lists, load_sems = scratch[:6]
    scratch = scratch[6:]
    loads = [
        pltpu.make_async_copy(operands[k], scratch_ref, load_sems.at[k])
        for k, scratch_ref in enumerate((tracers, weights, owners, slots, lists))
    ]
    for load in loads:
        load.start()
    received = scratch[:count]
    fields = scratch[count : count + chunks]
    (sending, mixing, source, moved, tile_out, tile_in, face_out, face_in,
     list_send, list_recv, tile_send, tile_recv, face_send, face_recv) = scratch[count + chunks :]

    face, tile = lax.axis_index("face"), lax.axis_index("tile")
    n_face, n_tile = lax.axis_size("face"), lax.axis_size("tile")
    south = (lax.rem(face + 1, n_face), tile)
    north = (lax.rem(face + n_face - 1, n_face), tile)
    east = (face, lax.rem(tile + 1, n_tile))
    west = (face, lax.rem(tile + n_tile - 1, n_tile))
    toward = (south, north, east, west)

    barrier = pltpu.get_barrier_semaphore()
    for device in toward:
        pl.semaphore_signal(barrier, inc=1, device_id=device, device_id_type=MESH)
    pl.semaphore_wait(barrier, 4)
    for load in loads:
        load.wait()

    def list_copy(s, c, j):
        return pltpu.make_async_remote_copy(
            src_ref=sending.at[s, c, j],
            dst_ref=received[s * chunks + c].at[j],
            send_sem=list_send.at[s, c, j],
            recv_sem=list_recv.at[s, c, j],
            device_id=toward[j],
            device_id_type=MESH,
        )

    def edge_copy(s, c, j):
        store, land, send, recv = (
            (tile_out, tile_in, tile_send, tile_recv)
            if j >= 2
            else (face_out, face_in, face_send, face_recv)
        )
        return pltpu.make_async_remote_copy(
            src_ref=store.at[s, c, j % 2],
            dst_ref=land.at[s, c, j % 2],
            send_sem=send.at[s, c, j % 2],
            recv_sem=recv.at[s, c, j % 2],
            device_id=toward[j],
            device_id_type=MESH,
        )

    def columns(c):
        return slice(c * width, (c + 1) * width)

    def field_block(s, c, elem):
        if s == 0:
            return tracers[elem, :, columns(c)]
        return fields[c][elem]

    def send_lists(s, c):
        for j in range(4):
            def pick(k, carry, j=j):
                elem = lists[s, 4 * face + j, tile * cap + k]
                sending[s, c, j, k] = field_block(s, c, elem)
                return carry
            lax.fori_loop(0, cap, pick, 0, unroll=True)
            list_copy(s, c, j).start()

    for c in range(min(AHEAD, chunks)):
        send_lists(0, c)

    lane = lax.broadcasted_iota(jnp.int32, (NODES, rows), 1)
    spread = jnp.where(
        (lane & (NODES - 1)) == lax.broadcasted_iota(jnp.int32, (NODES, rows), 0), 1.0, 0.0
    ).astype(jnp.float32)
    same = (lax.broadcasted_iota(jnp.int32, (rows, rows), 0) // NODES) == (
        lax.broadcasted_iota(jnp.int32, (rows, rows), 1) // NODES
    )
    for s in range(steps):
        repeated = jnp.dot(
            weights[s], spread, precision=HIGHEST, preferred_element_type=jnp.float32
        )
        high, low = halves(jnp.where(same, repeated, 0.0))
        mixing[s] = jnp.concatenate([high, low, high], axis=1)

    node = lax.broadcasted_iota(jnp.int32, (NODES, width), 0)
    flat_node = lax.broadcasted_iota(jnp.int32, (rows, width), 0) & (NODES - 1)

    def shift(block, amount):
        amount = amount % block.shape[0]
        return pltpu.roll(block, amount, 0) if amount else block

    def grid_of(flat):
        return flat.reshape(side, side, NODES, width)

    def pack(blocks, shifts, place):
        packed = shift(blocks[0], shifts[0])
        for k in range(1, side):
            packed = jnp.where(place == k, shift(blocks[k], shifts[k]), packed)
        return packed

    def interpolate(s, c):
        for j in range(4):
            list_copy(s, c, j).wait_recv()
        if s == 0 and c + AHEAD < chunks:
            send_lists(0, c + AHEAD)
        arrived = received[s * chunks + c]

        def pick(elem, carry):
            owner = owners[s, elem // side, elem % side]
            slot = slots[s, elem // side, elem % side]
            own = field_block(s, c, slot)
            other = arrived[jnp.maximum(owner - 1, 0), jnp.minimum(slot, cap - 1)]
            source[elem] = jnp.where(owner == 0, own, other)
            return carry

        lax.fori_loop(0, elems, pick, 0, unroll=True)
        blocks = source[...]
        high, low = halves(blocks.reshape(rows, width))
        mixed = jnp.dot(
            mixing[s],
            jnp.concatenate([high, high, low], axis=0),
            preferred_element_type=jnp.float32,
        ).reshape(elems, NODES, width)
        mixed = jnp.clip(
            mixed, jnp.min(blocks, axis=1, keepdims=True), jnp.max(blocks, axis=1, keepdims=True)
        )
        moved[c] = mixed
        grid = mixed.reshape(side, side, NODES, width)
        place = node & 3
        tile_out[s, c, 0] = pack(
            [grid[x, side - 1] for x in range(side)], [x - 3 for x in range(side)], place
        )
        tile_out[s, c, 1] = pack([grid[x, 0] for x in range(side)], list(range(side)), place)
        edge_copy(s, c, 2).start()
        edge_copy(s, c, 3).start()

    def average(flat, before, after, low, high, hop):
        return jnp.where(
            low,
            0.5 * (flat + shift(before, -hop)),
            jnp.where(high, 0.5 * (flat + shift(after, hop)), flat),
        )

    def average_columns(s, c):
        edge_copy(s, c, 2).wait_recv()
        edge_copy(s, c, 3).wait_recv()
        flat = moved[c].reshape(rows, width)
        grid = grid_of(flat)
        from_west, from_east = tile_in[s, c, 0], tile_in[s, c, 1]
        left = jnp.stack([shift(from_west, 3 - x) for x in range(side)])[:, None]
        right = jnp.stack([shift(from_east, -x) for x in range(side)])[:, None]
        before = jnp.concatenate([left, grid[:, : side - 1]], axis=1).reshape(rows, width)
        after = jnp.concatenate([grid[:, 1:], right], axis=1).reshape(rows, width)
        flat = average(flat, before, after, (flat_node & 3) == 0, (flat_node & 3) == 3, 3)
        moved[c] = flat.reshape(elems, NODES, width)
        grid = grid_of(flat)
        place = node >> 2
        face_out[s, c, 0] = pack(
            [grid[side - 1, y] for y in range(side)], [4 * y - 12 for y in range(side)], place
        )
        face_out[s, c, 1] = pack(
            [grid[0, y] for y in range(side)], [4 * y for y in range(side)], place
        )
        edge_copy(s, c, 0).start()
        edge_copy(s, c, 1).start()

    def average_rows(s, c):
        edge_copy(s, c, 0).wait_recv()
        edge_copy(s, c, 1).wait_recv()
        flat = moved[c].reshape(rows, width)
        grid = grid_of(flat)
        from_north, from_south = face_in[s, c, 0], face_in[s, c, 1]
        above = jnp.stack([shift(from_north, 12 - 4 * y) for y in range(side)])[None]
        below = jnp.stack([shift(from_south, -4 * y) for y in range(side)])[None]
        before = jnp.concatenate([above, grid[: side - 1]], axis=0).reshape(rows, width)
        after = jnp.concatenate([grid[1:], below], axis=0).reshape(rows, width)
        flat = average(flat, before, after, flat_node < 4, flat_node >= 12, 12)
        if s < steps - 1:
            fields[c][...] = flat.reshape(elems, NODES, width)
            send_lists(s + 1, c)
        else:
            out[:, :, columns(c)] = flat.reshape(elems, NODES, width)

    phases = (interpolate, average_columns, average_rows)
    for turn in range(chunks + SLACK * (3 * steps - 1)):
        for s in range(steps):
            for phase in (2, 1, 0):
                c = turn - SLACK * (3 * s + phase)
                if 0 <= c < chunks:
                    phases[phase](s, c)

    for s in range(steps):
        for c in range(chunks):
            for j in range(4):
                list_copy(s, c, j).wait_send()
                edge_copy(s, c, j).wait_send()


def local(tracers, basis_weights, up_owner, up_slot, send_list):
    side = tracers.shape[0]
    columns = tracers.shape[3]
    steps = basis_weights.shape[0]
    elems = side * side
    rows = elems * NODES
    cap = send_list.shape[2] // lax.axis_size("tile")
    width = chunk_width(columns)
    chunks = columns // width
    dims = (steps, side, cap, chunks, width)
    vmem = pl.BlockSpec(memory_space=pltpu.VMEM)
    whole = pl.BlockSpec(memory_space=pltpu.HBM)
    f32 = jnp.float32
    edges = pltpu.VMEM((steps, chunks, 2, NODES, width), f32)
    list_sems = pltpu.SemaphoreType.DMA((steps, chunks, 4))
    edge_sems = pltpu.SemaphoreType.DMA((steps, chunks, 2))
    result = pl.pallas_call(
        functools.partial(kernel, dims),
        out_shape=jax.ShapeDtypeStruct((elems, NODES, columns), f32),
        in_specs=[whole] * 5,
        out_specs=vmem,
        scratch_shapes=[
            pltpu.VMEM((elems, NODES, columns), f32),
            pltpu.VMEM((steps, rows, NODES), f32),
            pltpu.SMEM(up_owner.shape, jnp.int32),
            pltpu.SMEM(up_slot.shape, jnp.int32),
            pltpu.SMEM(send_list.shape, jnp.int32),
            pltpu.SemaphoreType.DMA((5,)),
        ]
        + [pltpu.VMEM((4, cap, NODES, width), f32)] * (steps * chunks)
        + [pltpu.VMEM((elems, NODES, width), f32)] * chunks
        + [
            pltpu.VMEM((steps, chunks, 4, cap, NODES, width), f32),
            pltpu.VMEM((steps, rows, 3 * rows), jnp.bfloat16),
            pltpu.VMEM((elems, NODES, width), f32),
            pltpu.VMEM((chunks, elems, NODES, width), f32),
            edges,
            edges,
            edges,
            edges,
            list_sems,
            list_sems,
            edge_sems,
            edge_sems,
            edge_sems,
            edge_sems,
        ],
        compiler_params=pltpu.CompilerParams(
            collective_id=0, has_side_effects=True, vmem_limit_bytes=40 * 1024 * 1024
        ),
        cost_estimate=pl.CostEstimate(
            flops=2 * steps * rows * NODES * columns,
            bytes_accessed=8 * rows * columns,
            transcendentals=0,
        ),
    )(
        tracers.reshape(elems, NODES, columns),
        basis_weights.reshape(steps, rows, NODES),
        up_owner,
        up_slot,
        send_list,
    )
    return result.reshape(side, side, NODES, columns)


def solution(mesh):
    return jax.shard_map(
        local,
        mesh=mesh,
        in_specs=(
            P("face", "tile", None, None),
            P(None, "face", "tile", None, None),
            P(None, "face", "tile"),
            P(None, "face", "tile"),
            P(),
        ),
        out_specs=P("face", "tile", None, None),
        check_vma=False,
    )
```

```python
import functools

import jax
import jax.numpy as jnp
from jax import lax
from jax.experimental import pallas as pl
from jax.experimental.pallas import tpu as pltpu
from jax.sharding import PartitionSpec as P

MESH = pl.DeviceIdType.MESH
NODES = 16
SLACK = 2
AHEAD = 3
HIGHEST = lax.Precision.HIGHEST


def chunk_width(columns):
    for width in (256, 128):
        if columns % width == 0:
            return width
    return columns


def halves(values):
    high = values.astype(jnp.bfloat16)
    return high, (values - high.astype(jnp.float32)).astype(jnp.bfloat16)


def kernel(dims, *refs):
    steps, side, cap, chunks, width = dims
    elems = side * side
    rows = elems * NODES
    operands, out, scratch = refs[:5], refs[5], refs[6:]
    (fields, weights, owners, slots, lists, load_sems, received, arrived, sending, mixing,
     source, moved, tile_out, tile_in, face_out, face_in,
     list_send, list_recv, tile_send, tile_recv, face_send, face_recv) = scratch
    loads = [
        pltpu.make_async_copy(
            operands[0].at[:, :, pl.ds(c * width, width)], fields.at[0, c], load_sems.at[4 + c]
        )
        for c in range(chunks)
    ]
    loads += [
        pltpu.make_async_copy(operands[1 + k], ref, load_sems.at[k])
        for k, ref in enumerate((weights, owners, slots, lists))
    ]
    for load in loads:
        load.start()

    face, tile = lax.axis_index("face"), lax.axis_index("tile")
    n_face, n_tile = lax.axis_size("face"), lax.axis_size("tile")
    south = (lax.rem(face + 1, n_face), tile)
    north = (lax.rem(face + n_face - 1, n_face), tile)
    east = (face, lax.rem(tile + 1, n_tile))
    west = (face, lax.rem(tile + n_tile - 1, n_tile))
    toward = (south, north, east, west)

    barrier = pltpu.get_barrier_semaphore()
    for device in toward:
        pl.semaphore_signal(barrier, inc=1, device_id=device, device_id_type=MESH)
    pl.semaphore_wait(barrier, 4)
    for load in loads:
        load.wait()

    def list_copy(s, c, j):
        return pltpu.make_async_remote_copy(
            src_ref=sending.at[s, c, j],
            dst_ref=received.at[s, c, j],
            send_sem=list_send.at[s, c, j],
            recv_sem=list_recv.at[s, c, j],
            device_id=toward[j],
            device_id_type=MESH,
        )

    def edge_copy(s, c, j):
        store, land, send, recv = (
            (tile_out, tile_in, tile_send, tile_recv)
            if j >= 2
            else (face_out, face_in, face_send, face_recv)
        )
        return pltpu.make_async_remote_copy(
            src_ref=store.at[s, c, j % 2],
            dst_ref=land.at[s, c, j % 2],
            send_sem=send.at[s, c, j % 2],
            recv_sem=recv.at[s, c, j % 2],
            device_id=toward[j],
            device_id_type=MESH,
        )

    def send_lists(s, c):
        for j in range(4):
            def pick(k, carry, j=j):
                elem = lists[s, 4 * face + j, tile * cap + k]
                sending[s, c, j, k] = fields[s, c, elem]
                return carry
            lax.fori_loop(0, cap, pick, 0, unroll=True)
            list_copy(s, c, j).start()

    def send_first(c, carry):
        send_lists(0, c)
        return carry

    ahead = min(AHEAD, chunks)
    lax.fori_loop(0, ahead, send_first, 0)

    lane = lax.broadcasted_iota(jnp.int32, (NODES, rows), 1)
    spread = jnp.where(
        (lane & (NODES - 1)) == lax.broadcasted_iota(jnp.int32, (NODES, rows), 0), 1.0, 0.0
    ).astype(jnp.float32)
    same = (lax.broadcasted_iota(jnp.int32, (rows, rows), 0) // NODES) == (
        lax.broadcasted_iota(jnp.int32, (rows, rows), 1) // NODES
    )
    def build(s, carry):
        repeated = jnp.dot(
            weights[s], spread, precision=HIGHEST, preferred_element_type=jnp.float32
        )
        high, low = halves(jnp.where(same, repeated, 0.0))
        mixing[s] = jnp.concatenate([high, low, high], axis=1)
        return carry

    lax.fori_loop(0, steps, build, 0)

    node = lax.broadcasted_iota(jnp.int32, (NODES, width), 0)
    flat_node = lax.broadcasted_iota(jnp.int32, (rows, width), 0) & (NODES - 1)

    def shift(block, amount):
        amount = amount % block.shape[0]
        return pltpu.roll(block, amount, 0) if amount else block

    def grid_of(flat):
        return flat.reshape(side, side, NODES, width)

    def pack(blocks, shifts, place):
        packed = shift(blocks[0], shifts[0])
        for k in range(1, side):
            packed = jnp.where(place == k, shift(blocks[k], shifts[k]), packed)
        return packed

    def interpolate(s, c):
        for j in range(4):
            list_copy(s, c, j).wait_recv()

        @pl.when((s == 0) & (c + ahead < chunks))
        def _():
            send_lists(0, c + ahead)

        arrived[...] = received[s, c]

        def pick(elem, carry):
            owner = owners[s, elem // side, elem % side]
            slot = slots[s, elem // side, elem % side]
            own = fields[s, c, slot]
            other = arrived[jnp.maximum(owner - 1, 0), jnp.minimum(slot, cap - 1)]
            source[elem] = jnp.where(owner == 0, own, other)
            return carry

        lax.fori_loop(0, elems, pick, 0, unroll=True)
        blocks = source[...]
        high, low = halves(blocks.reshape(rows, width))
        mixed = jnp.dot(
            mixing[s],
            jnp.concatenate([high, high, low], axis=0),
            preferred_element_type=jnp.float32,
        ).reshape(elems, NODES, width)
        mixed = jnp.clip(
            mixed, jnp.min(blocks, axis=1, keepdims=True), jnp.max(blocks, axis=1, keepdims=True)
        )
        moved[c] = mixed
        grid = mixed.reshape(side, side, NODES, width)
        place = node & 3
        tile_out[s, c, 0] = pack(
            [grid[x, side - 1] for x in range(side)], [x - 3 for x in range(side)], place
        )
        tile_out[s, c, 1] = pack([grid[x, 0] for x in range(side)], list(range(side)), place)
        edge_copy(s, c, 2).start()
        edge_copy(s, c, 3).start()

    def average(flat, before, after, low, high, hop):
        return jnp.where(
            low,
            0.5 * (flat + shift(before, -hop)),
            jnp.where(high, 0.5 * (flat + shift(after, hop)), flat),
        )

    def average_columns(s, c):
        edge_copy(s, c, 2).wait_recv()
        edge_copy(s, c, 3).wait_recv()
        flat = moved[c].reshape(rows, width)
        grid = grid_of(flat)
        from_west, from_east = tile_in[s, c, 0], tile_in[s, c, 1]
        left = jnp.stack([shift(from_west, 3 - x) for x in range(side)])[:, None]
        right = jnp.stack([shift(from_east, -x) for x in range(side)])[:, None]
        before = jnp.concatenate([left, grid[:, : side - 1]], axis=1).reshape(rows, width)
        after = jnp.concatenate([grid[:, 1:], right], axis=1).reshape(rows, width)
        flat = average(flat, before, after, (flat_node & 3) == 0, (flat_node & 3) == 3, 3)
        moved[c] = flat.reshape(elems, NODES, width)
        grid = grid_of(flat)
        place = node >> 2
        face_out[s, c, 0] = pack(
            [grid[side - 1, y] for y in range(side)], [4 * y - 12 for y in range(side)], place
        )
        face_out[s, c, 1] = pack(
            [grid[0, y] for y in range(side)], [4 * y for y in range(side)], place
        )
        edge_copy(s, c, 0).start()
        edge_copy(s, c, 1).start()

    def average_rows(s, c):
        edge_copy(s, c, 0).wait_recv()
        edge_copy(s, c, 1).wait_recv()
        flat = moved[c].reshape(rows, width)
        grid = grid_of(flat)
        from_north, from_south = face_in[s, c, 0], face_in[s, c, 1]
        above = jnp.stack([shift(from_north, 12 - 4 * y) for y in range(side)])[None]
        below = jnp.stack([shift(from_south, -4 * y) for y in range(side)])[None]
        before = jnp.concatenate([above, grid[: side - 1]], axis=0).reshape(rows, width)
        after = jnp.concatenate([grid[1:], below], axis=0).reshape(rows, width)
        flat = average(flat, before, after, flat_node < 4, flat_node >= 12, 12)
        averaged = flat.reshape(elems, NODES, width)

        @pl.when(s < steps - 1)
        def _():
            fields[s + 1, c] = averaged
            send_lists(s + 1, c)

        @pl.when(s == steps - 1)
        def _():
            out[:, :, pl.ds(pl.multiple_of(c * width, width), width)] = averaged

    phases = (interpolate, average_columns, average_rows)
    def advance(turn, carry):
        def advance_step(s, carry):
            for phase in (2, 1, 0):
                c = turn - SLACK * (3 * s + phase)

                @pl.when((c >= 0) & (c < chunks))
                def _():
                    phases[phase](s, c)

            return carry

        return lax.fori_loop(0, steps, advance_step, carry)

    lax.fori_loop(0, chunks + SLACK * (3 * steps - 1), advance, 0)

    def finish(k, carry):
        s, c = k // chunks, k % chunks
        for j in range(4):
            list_copy(s, c, j).wait_send()
            edge_copy(s, c, j).wait_send()
        return carry

    lax.fori_loop(0, steps * chunks, finish, 0)


def local(tracers, basis_weights, up_owner, up_slot, send_list):
    side = tracers.shape[0]
    columns = tracers.shape[3]
    steps = basis_weights.shape[0]
    elems = side * side
    rows = elems * NODES
    cap = send_list.shape[2] // lax.axis_size("tile")
    width = chunk_width(columns)
    chunks = columns // width
    dims = (steps, side, cap, chunks, width)
    vmem = pl.BlockSpec(memory_space=pltpu.VMEM)
    whole = pl.BlockSpec(memory_space=pltpu.HBM)
    f32 = jnp.float32
    edges = pltpu.VMEM((steps, chunks, 2, NODES, width), f32)
    list_sems = pltpu.SemaphoreType.DMA((steps, chunks, 4))
    edge_sems = pltpu.SemaphoreType.DMA((steps, chunks, 2))
    result = pl.pallas_call(
        functools.partial(kernel, dims),
        out_shape=jax.ShapeDtypeStruct((elems, NODES, columns), f32),
        in_specs=[whole] * 5,
        out_specs=vmem,
        scratch_shapes=[
            pltpu.VMEM((steps, chunks, elems, NODES, width), f32),
            pltpu.VMEM((steps, rows, NODES), f32),
            pltpu.SMEM(up_owner.shape, jnp.int32),
            pltpu.SMEM(up_slot.shape, jnp.int32),
            pltpu.SMEM(send_list.shape, jnp.int32),
            pltpu.SemaphoreType.DMA((4 + chunks,)),
            pltpu.VMEM((steps, chunks, 4, cap, NODES, width), f32),
            pltpu.VMEM((4, cap, NODES, width), f32),
            pltpu.VMEM((steps, chunks, 4, cap, NODES, width), f32),
            pltpu.VMEM((steps, rows, 3 * rows), jnp.bfloat16),
            pltpu.VMEM((elems, NODES, width), f32),
            pltpu.VMEM((chunks, elems, NODES, width), f32),
            edges,
            edges,
            edges,
            edges,
            list_sems,
            list_sems,
            edge_sems,
            edge_sems,
            edge_sems,
            edge_sems,
        ],
        compiler_params=pltpu.CompilerParams(
            collective_id=0, has_side_effects=True, vmem_limit_bytes=62 * 1024 * 1024
        ),
        cost_estimate=pl.CostEstimate(
            flops=2 * steps * rows * NODES * columns,
            bytes_accessed=8 * rows * columns,
            transcendentals=0,
        ),
    )(
        tracers.reshape(elems, NODES, columns),
        basis_weights.reshape(steps, rows, NODES),
        up_owner,
        up_slot,
        send_list,
    )
    return result.reshape(side, side, NODES, columns)


def solution(mesh):
    return jax.shard_map(
        local,
        mesh=mesh,
        in_specs=(
            P("face", "tile", None, None),
            P(None, "face", "tile", None, None),
            P(None, "face", "tile"),
            P(None, "face", "tile"),
            P(),
        ),
        out_specs=P("face", "tile", None, None),
        check_vma=False,
    )
```

```python
import functools

import jax
import jax.numpy as jnp
from jax import lax
from jax.experimental import pallas as pl
from jax.experimental.pallas import tpu as pltpu
from jax.sharding import PartitionSpec as P

MESH = pl.DeviceIdType.MESH
NODES = 16
SLACK = 2
AHEAD = 4
HIGHEST = lax.Precision.HIGHEST


def chunk_width(columns):
    return 128 if columns % 128 == 0 else columns


def halves(values):
    high = values.astype(jnp.bfloat16)
    return high, (values - high.astype(jnp.float32)).astype(jnp.bfloat16)


def kernel(dims, *refs):
    steps, side, cap, chunks, width = dims
    elems = side * side
    rows = elems * NODES
    operands, out, scratch = refs[:5], refs[5], refs[6:]
    (fields, weights, owners, slots, lists, load_sems, received, arrived, sending, mixing,
     source, moved, tile_out, tile_in, face_out, face_in,
     list_send, list_recv, tile_send, tile_recv, face_send, face_recv) = scratch
    loads = [
        pltpu.make_async_copy(
            operands[0].at[:, :, pl.ds(c * width, width)], fields.at[0, c], load_sems.at[4 + c]
        )
        for c in range(chunks)
    ]
    loads += [
        pltpu.make_async_copy(operands[1 + k], ref, load_sems.at[k])
        for k, ref in enumerate((weights, owners, slots, lists))
    ]
    for load in loads:
        load.start()

    face, tile = lax.axis_index("face"), lax.axis_index("tile")
    n_face, n_tile = lax.axis_size("face"), lax.axis_size("tile")
    south = (lax.rem(face + 1, n_face), tile)
    north = (lax.rem(face + n_face - 1, n_face), tile)
    east = (face, lax.rem(tile + 1, n_tile))
    west = (face, lax.rem(tile + n_tile - 1, n_tile))
    toward = (south, north, east, west)

    barrier = pltpu.get_barrier_semaphore()
    for device in toward:
        pl.semaphore_signal(barrier, inc=1, device_id=device, device_id_type=MESH)
    pl.semaphore_wait(barrier, 4)
    for load in loads:
        load.wait()

    def list_copy(s, c, j):
        return pltpu.make_async_remote_copy(
            src_ref=sending.at[s, c, j],
            dst_ref=received.at[s, c, j],
            send_sem=list_send.at[s, c, j],
            recv_sem=list_recv.at[s, c, j],
            device_id=toward[j],
            device_id_type=MESH,
        )

    def edge_copy(s, c, j):
        store, land, send, recv = (
            (tile_out, tile_in, tile_send, tile_recv)
            if j >= 2
            else (face_out, face_in, face_send, face_recv)
        )
        return pltpu.make_async_remote_copy(
            src_ref=store.at[s, c, j % 2],
            dst_ref=land.at[s, c, j % 2],
            send_sem=send.at[s, c, j % 2],
            recv_sem=recv.at[s, c, j % 2],
            device_id=toward[j],
            device_id_type=MESH,
        )

    def send_lists(s, c):
        for j in range(4):
            def pick(k, carry, j=j):
                elem = lists[s, 4 * face + j, tile * cap + k]
                sending[s, c, j, k] = fields[s, c, elem]
                return carry
            lax.fori_loop(0, cap, pick, 0, unroll=True)
            list_copy(s, c, j).start()

    def send_first(c, carry):
        send_lists(0, c)
        return carry

    ahead = min(AHEAD, chunks)
    lax.fori_loop(0, ahead, send_first, 0)

    lane = lax.broadcasted_iota(jnp.int32, (NODES, rows), 1)
    spread = jnp.where(
        (lane & (NODES - 1)) == lax.broadcasted_iota(jnp.int32, (NODES, rows), 0), 1.0, 0.0
    ).astype(jnp.float32)
    same = (lax.broadcasted_iota(jnp.int32, (rows, rows), 0) // NODES) == (
        lax.broadcasted_iota(jnp.int32, (rows, rows), 1) // NODES
    )
    def build(s, carry):
        repeated = jnp.dot(
            weights[s], spread, precision=HIGHEST, preferred_element_type=jnp.float32
        )
        high, low = halves(jnp.where(same, repeated, 0.0))
        mixing[s] = jnp.concatenate([high, low, high], axis=1)
        return carry

    lax.fori_loop(0, steps, build, 0)

    node = lax.broadcasted_iota(jnp.int32, (NODES, width), 0)
    flat_node = lax.broadcasted_iota(jnp.int32, (rows, width), 0) & (NODES - 1)

    def shift(block, amount):
        amount = amount % block.shape[0]
        return pltpu.roll(block, amount, 0) if amount else block

    def grid_of(flat):
        return flat.reshape(side, side, NODES, width)

    def pack(blocks, shifts, place):
        packed = shift(blocks[0], shifts[0])
        for k in range(1, side):
            packed = jnp.where(place == k, shift(blocks[k], shifts[k]), packed)
        return packed

    def interpolate(s, c):
        for j in range(4):
            list_copy(s, c, j).wait_recv()

        @pl.when((s == 0) & (c + ahead < chunks))
        def _():
            send_lists(0, c + ahead)

        arrived[...] = received[s, c]

        def pick(elem, carry):
            owner = owners[s, elem // side, elem % side]
            slot = slots[s, elem // side, elem % side]
            own = fields[s, c, slot]
            other = arrived[jnp.maximum(owner - 1, 0), jnp.minimum(slot, cap - 1)]
            source[elem] = jnp.where(owner == 0, own, other)
            return carry

        lax.fori_loop(0, elems, pick, 0, unroll=True)
        blocks = source[...]
        high, low = halves(blocks.reshape(rows, width))
        mixed = jnp.dot(
            mixing[s],
            jnp.concatenate([high, high, low], axis=0),
            preferred_element_type=jnp.float32,
        ).reshape(elems, NODES, width)
        mixed = jnp.clip(
            mixed, jnp.min(blocks, axis=1, keepdims=True), jnp.max(blocks, axis=1, keepdims=True)
        )
        moved[c] = mixed
        grid = mixed.reshape(side, side, NODES, width)
        place = node & 3
        tile_out[s, c, 0] = pack(
            [grid[x, side - 1] for x in range(side)], [x - 3 for x in range(side)], place
        )
        tile_out[s, c, 1] = pack([grid[x, 0] for x in range(side)], list(range(side)), place)
        edge_copy(s, c, 2).start()
        edge_copy(s, c, 3).start()

    def average(flat, before, after, low, high, hop):
        return jnp.where(
            low,
            0.5 * (flat + shift(before, -hop)),
            jnp.where(high, 0.5 * (flat + shift(after, hop)), flat),
        )

    def average_columns(s, c):
        edge_copy(s, c, 2).wait_recv()
        edge_copy(s, c, 3).wait_recv()
        flat = moved[c].reshape(rows, width)
        grid = grid_of(flat)
        from_west, from_east = tile_in[s, c, 0], tile_in[s, c, 1]
        left = jnp.stack([shift(from_west, 3 - x) for x in range(side)])[:, None]
        right = jnp.stack([shift(from_east, -x) for x in range(side)])[:, None]
        before = jnp.concatenate([left, grid[:, : side - 1]], axis=1).reshape(rows, width)
        after = jnp.concatenate([grid[:, 1:], right], axis=1).reshape(rows, width)
        flat = average(flat, before, after, (flat_node & 3) == 0, (flat_node & 3) == 3, 3)
        moved[c] = flat.reshape(elems, NODES, width)
        grid = grid_of(flat)
        place = node >> 2
        face_out[s, c, 0] = pack(
            [grid[side - 1, y] for y in range(side)], [4 * y - 12 for y in range(side)], place
        )
        face_out[s, c, 1] = pack(
            [grid[0, y] for y in range(side)], [4 * y for y in range(side)], place
        )
        edge_copy(s, c, 0).start()
        edge_copy(s, c, 1).start()

    def average_rows(s, c):
        edge_copy(s, c, 0).wait_recv()
        edge_copy(s, c, 1).wait_recv()
        flat = moved[c].reshape(rows, width)
        grid = grid_of(flat)
        from_north, from_south = face_in[s, c, 0], face_in[s, c, 1]
        above = jnp.stack([shift(from_north, 12 - 4 * y) for y in range(side)])[None]
        below = jnp.stack([shift(from_south, -4 * y) for y in range(side)])[None]
        before = jnp.concatenate([above, grid[: side - 1]], axis=0).reshape(rows, width)
        after = jnp.concatenate([grid[1:], below], axis=0).reshape(rows, width)
        flat = average(flat, before, after, flat_node < 4, flat_node >= 12, 12)
        averaged = flat.reshape(elems, NODES, width)

        @pl.when(s < steps - 1)
        def _():
            fields[s + 1, c] = averaged
            send_lists(s + 1, c)

        @pl.when(s == steps - 1)
        def _():
            out[:, :, pl.ds(pl.multiple_of(c * width, width), width)] = averaged

    phases = (interpolate, average_columns, average_rows)
    def advance(turn, carry):
        def advance_step(s, carry):
            for phase in (2, 1, 0):
                c = turn - SLACK * (3 * s + phase)

                @pl.when((c >= 0) & (c < chunks))
                def _():
                    phases[phase](s, c)

            return carry

        return lax.fori_loop(0, steps, advance_step, carry)

    lax.fori_loop(0, chunks + SLACK * (3 * steps - 1), advance, 0)

    def finish(k, carry):
        s, c = k // chunks, k % chunks
        for j in range(4):
            list_copy(s, c, j).wait_send()
            edge_copy(s, c, j).wait_send()
        return carry

    lax.fori_loop(0, steps * chunks, finish, 0)


def local(tracers, basis_weights, up_owner, up_slot, send_list):
    side = tracers.shape[0]
    columns = tracers.shape[3]
    steps = basis_weights.shape[0]
    elems = side * side
    rows = elems * NODES
    cap = send_list.shape[2] // lax.axis_size("tile")
    width = chunk_width(columns)
    chunks = columns // width
    dims = (steps, side, cap, chunks, width)
    vmem = pl.BlockSpec(memory_space=pltpu.VMEM)
    whole = pl.BlockSpec(memory_space=pltpu.HBM)
    f32 = jnp.float32
    edges = pltpu.VMEM((steps, chunks, 2, NODES, width), f32)
    list_sems = pltpu.SemaphoreType.DMA((steps, chunks, 4))
    edge_sems = pltpu.SemaphoreType.DMA((steps, chunks, 2))
    result = pl.pallas_call(
        functools.partial(kernel, dims),
        out_shape=jax.ShapeDtypeStruct((elems, NODES, columns), f32),
        in_specs=[whole] * 5,
        out_specs=vmem,
        scratch_shapes=[
            pltpu.VMEM((steps, chunks, elems, NODES, width), f32),
            pltpu.VMEM((steps, rows, NODES), f32),
            pltpu.SMEM(up_owner.shape, jnp.int32),
            pltpu.SMEM(up_slot.shape, jnp.int32),
            pltpu.SMEM(send_list.shape, jnp.int32),
            pltpu.SemaphoreType.DMA((4 + chunks,)),
            pltpu.VMEM((steps, chunks, 4, cap, NODES, width), f32),
            pltpu.VMEM((4, cap, NODES, width), f32),
            pltpu.VMEM((steps, chunks, 4, cap, NODES, width), f32),
            pltpu.VMEM((steps, rows, 3 * rows), jnp.bfloat16),
            pltpu.VMEM((elems, NODES, width), f32),
            pltpu.VMEM((chunks, elems, NODES, width), f32),
            edges,
            edges,
            edges,
            edges,
            list_sems,
            list_sems,
            edge_sems,
            edge_sems,
            edge_sems,
            edge_sems,
        ],
        compiler_params=pltpu.CompilerParams(
            collective_id=0, has_side_effects=True, vmem_limit_bytes=62 * 1024 * 1024
        ),
        cost_estimate=pl.CostEstimate(
            flops=2 * steps * rows * NODES * columns,
            bytes_accessed=8 * rows * columns,
            transcendentals=0,
        ),
    )(
        tracers.reshape(elems, NODES, columns),
        basis_weights.reshape(steps, rows, NODES),
        up_owner,
        up_slot,
        send_list,
    )
    return result.reshape(side, side, NODES, columns)


def solution(mesh):
    return jax.shard_map(
        local,
        mesh=mesh,
        in_specs=(
            P("face", "tile", None, None),
            P(None, "face", "tile", None, None),
            P(None, "face", "tile"),
            P(None, "face", "tile"),
            P(),
        ),
        out_specs=P("face", "tile", None, None),
        check_vma=False,
    )
```

```python
import functools

import jax
import jax.numpy as jnp
from jax import lax
from jax.experimental import pallas as pl
from jax.experimental.pallas import tpu as pltpu
from jax.sharding import PartitionSpec as P

MESH = pl.DeviceIdType.MESH
NODES = 16
AHEAD = 3
HIGHEST = lax.Precision.HIGHEST


def chunk_width(columns):
    for width in (256, 128):
        if columns % width == 0:
            return width
    return columns


def halves(values):
    high = values.astype(jnp.bfloat16)
    return high, (values - high.astype(jnp.float32)).astype(jnp.bfloat16)


def kernel(dims, *refs):
    steps, side, cap, chunks, width = dims
    elems = side * side
    rows = elems * NODES
    operands, out, scratch = refs[:5], refs[5], refs[6:]
    (fields, weights, owners, slots, lists, load_sems, received, arrived, sending, mixing,
     source, moved, tile_out, tile_in, face_out, face_in,
     list_send, list_recv, tile_send, tile_recv, face_send, face_recv) = scratch
    loads = [
        pltpu.make_async_copy(
            operands[0].at[:, :, pl.ds(c * width, width)], fields.at[0, c], load_sems.at[4 + c]
        )
        for c in range(chunks)
    ]
    loads += [
        pltpu.make_async_copy(operands[1 + k], ref, load_sems.at[k])
        for k, ref in enumerate((weights, owners, slots, lists))
    ]
    for load in loads:
        load.start()

    face, tile = lax.axis_index("face"), lax.axis_index("tile")
    n_face, n_tile = lax.axis_size("face"), lax.axis_size("tile")
    south = (lax.rem(face + 1, n_face), tile)
    north = (lax.rem(face + n_face - 1, n_face), tile)
    east = (face, lax.rem(tile + 1, n_tile))
    west = (face, lax.rem(tile + n_tile - 1, n_tile))
    toward = (south, north, east, west)

    barrier = pltpu.get_barrier_semaphore()
    for device in toward:
        pl.semaphore_signal(barrier, inc=1, device_id=device, device_id_type=MESH)
    pl.semaphore_wait(barrier, 4)
    for load in loads:
        load.wait()

    def store(c):
        return pltpu.make_async_copy(
            moved.at[c],
            out.at[:, :, pl.ds(pl.multiple_of(c * width, width), width)],
            load_sems.at[4 + chunks + c],
        )

    def list_copy(s, c, j):
        return pltpu.make_async_remote_copy(
            src_ref=sending.at[s, c, j],
            dst_ref=received.at[s, c, j],
            send_sem=list_send.at[s, c, j],
            recv_sem=list_recv.at[s, c, j],
            device_id=toward[j],
            device_id_type=MESH,
        )

    def edge_copy(s, c, j):
        store, land, send, recv = (
            (tile_out, tile_in, tile_send, tile_recv)
            if j >= 2
            else (face_out, face_in, face_send, face_recv)
        )
        return pltpu.make_async_remote_copy(
            src_ref=store.at[s, c, j % 2],
            dst_ref=land.at[s, c, j % 2],
            send_sem=send.at[s, c, j % 2],
            recv_sem=recv.at[s, c, j % 2],
            device_id=toward[j],
            device_id_type=MESH,
        )

    def send_lists(s, c):
        for j in range(4):
            def pick(k, carry, j=j):
                elem = lists[s, 4 * face + j, tile * cap + k]
                sending[s, c, j, k] = fields[s, c, elem]
                return carry
            lax.fori_loop(0, cap, pick, 0, unroll=True)
            list_copy(s, c, j).start()

    def send_first(c, carry):
        send_lists(0, c)
        return carry

    ahead = min(AHEAD, chunks)
    lax.fori_loop(0, ahead, send_first, 0)

    lane = lax.broadcasted_iota(jnp.int32, (NODES, rows), 1)
    spread = jnp.where(
        (lane & (NODES - 1)) == lax.broadcasted_iota(jnp.int32, (NODES, rows), 0), 1.0, 0.0
    ).astype(jnp.float32)
    same = (lax.broadcasted_iota(jnp.int32, (rows, rows), 0) // NODES) == (
        lax.broadcasted_iota(jnp.int32, (rows, rows), 1) // NODES
    )
    def build(s, carry):
        repeated = jnp.dot(
            weights[s], spread, precision=HIGHEST, preferred_element_type=jnp.float32
        )
        high, low = halves(jnp.where(same, repeated, 0.0))
        mixing[s] = jnp.concatenate([high, low, high], axis=1)
        return carry

    lax.fori_loop(0, steps, build, 0)

    node = lax.broadcasted_iota(jnp.int32, (NODES, width), 0)
    flat_node = lax.broadcasted_iota(jnp.int32, (rows, width), 0) & (NODES - 1)

    def shift(block, amount):
        amount = amount % block.shape[0]
        return pltpu.roll(block, amount, 0) if amount else block

    def grid_of(flat):
        return flat.reshape(side, side, NODES, width)

    def pack(blocks, shifts, place):
        packed = shift(blocks[0], shifts[0])
        for k in range(1, side):
            packed = jnp.where(place == k, shift(blocks[k], shifts[k]), packed)
        return packed

    def interpolate(s, c):
        for j in range(4):
            list_copy(s, c, j).wait_recv()

        @pl.when((s == 0) & (c + ahead < chunks))
        def _():
            send_lists(0, c + ahead)

        arrived[...] = received[s, c]

        def pick(elem, carry):
            owner = owners[s, elem // side, elem % side]
            slot = slots[s, elem // side, elem % side]
            own = fields[s, c, slot]
            other = arrived[jnp.maximum(owner - 1, 0), jnp.minimum(slot, cap - 1)]
            source[elem] = jnp.where(owner == 0, own, other)
            return carry

        lax.fori_loop(0, elems, pick, 0, unroll=True)
        blocks = source[...]
        high, low = halves(blocks.reshape(rows, width))
        mixed = jnp.dot(
            mixing[s],
            jnp.concatenate([high, high, low], axis=0),
            preferred_element_type=jnp.float32,
        ).reshape(elems, NODES, width)
        mixed = jnp.clip(
            mixed, jnp.min(blocks, axis=1, keepdims=True), jnp.max(blocks, axis=1, keepdims=True)
        )
        moved[c] = mixed
        grid = mixed.reshape(side, side, NODES, width)
        place = node & 3
        tile_out[s, c, 0] = pack(
            [grid[x, side - 1] for x in range(side)], [x - 3 for x in range(side)], place
        )
        tile_out[s, c, 1] = pack([grid[x, 0] for x in range(side)], list(range(side)), place)
        edge_copy(s, c, 2).start()
        edge_copy(s, c, 3).start()

    def average(flat, before, after, low, high, hop):
        return jnp.where(
            low,
            0.5 * (flat + shift(before, -hop)),
            jnp.where(high, 0.5 * (flat + shift(after, hop)), flat),
        )

    def average_columns(s, c):
        edge_copy(s, c, 2).wait_recv()
        edge_copy(s, c, 3).wait_recv()
        flat = moved[c].reshape(rows, width)
        grid = grid_of(flat)
        from_west, from_east = tile_in[s, c, 0], tile_in[s, c, 1]
        left = jnp.stack([shift(from_west, 3 - x) for x in range(side)])[:, None]
        right = jnp.stack([shift(from_east, -x) for x in range(side)])[:, None]
        before = jnp.concatenate([left, grid[:, : side - 1]], axis=1).reshape(rows, width)
        after = jnp.concatenate([grid[:, 1:], right], axis=1).reshape(rows, width)
        flat = average(flat, before, after, (flat_node & 3) == 0, (flat_node & 3) == 3, 3)
        moved[c] = flat.reshape(elems, NODES, width)
        grid = grid_of(flat)
        place = node >> 2
        face_out[s, c, 0] = pack(
            [grid[side - 1, y] for y in range(side)], [4 * y - 12 for y in range(side)], place
        )
        face_out[s, c, 1] = pack(
            [grid[0, y] for y in range(side)], [4 * y for y in range(side)], place
        )
        edge_copy(s, c, 0).start()
        edge_copy(s, c, 1).start()

    def average_rows(s, c):
        edge_copy(s, c, 0).wait_recv()
        edge_copy(s, c, 1).wait_recv()
        flat = moved[c].reshape(rows, width)
        grid = grid_of(flat)
        from_north, from_south = face_in[s, c, 0], face_in[s, c, 1]
        above = jnp.stack([shift(from_north, 12 - 4 * y) for y in range(side)])[None]
        below = jnp.stack([shift(from_south, -4 * y) for y in range(side)])[None]
        before = jnp.concatenate([above, grid[: side - 1]], axis=0).reshape(rows, width)
        after = jnp.concatenate([grid[1:], below], axis=0).reshape(rows, width)
        flat = average(flat, before, after, flat_node < 4, flat_node >= 12, 12)
        averaged = flat.reshape(elems, NODES, width)

        @pl.when(s < steps - 1)
        def _():
            fields[s + 1, c] = averaged
            send_lists(s + 1, c)

        @pl.when(s == steps - 1)
        def _():
            moved[c] = averaged
            store(c).start()

    phases = (interpolate, average_columns, average_rows)
    def advance(turn, carry):
        def advance_step(s, carry):
            for phase in (2, 1, 0):
                c = turn - chunks * (3 * s + phase)

                @pl.when((c >= 0) & (c < chunks))
                def _():
                    phases[phase](s, c)

            return carry

        return lax.fori_loop(0, steps, advance_step, carry)

    lax.fori_loop(0, chunks + chunks * (3 * steps - 1), advance, 0)

    def finish(k, carry):
        s, c = k // chunks, k % chunks
        for j in range(4):
            list_copy(s, c, j).wait_send()
            edge_copy(s, c, j).wait_send()
        return carry

    lax.fori_loop(0, steps * chunks, finish, 0)

    def finish_store(c, carry):
        store(c).wait()
        return carry

    lax.fori_loop(0, chunks, finish_store, 0)


def local(tracers, basis_weights, up_owner, up_slot, send_list):
    side = tracers.shape[0]
    columns = tracers.shape[3]
    steps = basis_weights.shape[0]
    elems = side * side
    rows = elems * NODES
    cap = send_list.shape[2] // lax.axis_size("tile")
    width = chunk_width(columns)
    chunks = columns // width
    dims = (steps, side, cap, chunks, width)
    whole = pl.BlockSpec(memory_space=pltpu.HBM)
    f32 = jnp.float32
    edges = pltpu.VMEM((steps, chunks, 2, NODES, width), f32)
    list_sems = pltpu.SemaphoreType.DMA((steps, chunks, 4))
    edge_sems = pltpu.SemaphoreType.DMA((steps, chunks, 2))
    result = pl.pallas_call(
        functools.partial(kernel, dims),
        out_shape=jax.ShapeDtypeStruct((elems, NODES, columns), f32),
        in_specs=[whole] * 5,
        out_specs=whole,
        scratch_shapes=[
            pltpu.VMEM((steps, chunks, elems, NODES, width), f32),
            pltpu.VMEM((steps, rows, NODES), f32),
            pltpu.SMEM(up_owner.shape, jnp.int32),
            pltpu.SMEM(up_slot.shape, jnp.int32),
            pltpu.SMEM(send_list.shape, jnp.int32),
            pltpu.SemaphoreType.DMA((4 + 2 * chunks,)),
            pltpu.VMEM((steps, chunks, 4, cap, NODES, width), f32),
            pltpu.VMEM((4, cap, NODES, width), f32),
            pltpu.VMEM((steps, chunks, 4, cap, NODES, width), f32),
            pltpu.VMEM((steps, rows, 3 * rows), jnp.bfloat16),
            pltpu.VMEM((elems, NODES, width), f32),
            pltpu.VMEM((chunks, elems, NODES, width), f32),
            edges,
            edges,
            edges,
            edges,
            list_sems,
            list_sems,
            edge_sems,
            edge_sems,
            edge_sems,
            edge_sems,
        ],
        compiler_params=pltpu.CompilerParams(
            collective_id=0, has_side_effects=True, vmem_limit_bytes=62 * 1024 * 1024
        ),
        cost_estimate=pl.CostEstimate(
            flops=2 * steps * rows * NODES * columns,
            bytes_accessed=8 * rows * columns,
            transcendentals=0,
        ),
    )(
        tracers.reshape(elems, NODES, columns),
        basis_weights.reshape(steps, rows, NODES),
        up_owner,
        up_slot,
        send_list,
    )
    return result.reshape(side, side, NODES, columns)


def solution(mesh):
    return jax.shard_map(
        local,
        mesh=mesh,
        in_specs=(
            P("face", "tile", None, None),
            P(None, "face", "tile", None, None),
            P(None, "face", "tile"),
            P(None, "face", "tile"),
            P(),
        ),
        out_specs=P("face", "tile", None, None),
        check_vma=False,
    )
```

```python
import functools

import jax
import jax.numpy as jnp
from jax import lax
from jax.experimental import pallas as pl
from jax.experimental.pallas import tpu as pltpu
from jax.sharding import PartitionSpec as P

MESH = pl.DeviceIdType.MESH
NODES = 16
AHEAD = 3
HIGHEST = lax.Precision.HIGHEST


def chunk_width(columns):
    for width in (256, 128):
        if columns % width == 0:
            return width
    return columns


def halves(values):
    high = values.astype(jnp.bfloat16)
    return high, (values - high.astype(jnp.float32)).astype(jnp.bfloat16)


def kernel(dims, *refs):
    steps, side, cap, chunks, width = dims
    elems = side * side
    rows = elems * NODES
    operands, out, scratch = refs[:5], refs[5], refs[6:]
    (fields, weights, owners, slots, lists, load_sems, received, arrived, sending, mixing,
     source, tile_out, tile_in, face_out, face_in,
     list_send, list_recv, tile_send, tile_recv, face_send, face_recv) = scratch
    loads = [
        pltpu.make_async_copy(
            operands[0].at[:, :, pl.ds(c * width, width)], fields.at[0, c], load_sems.at[4 + c]
        )
        for c in range(chunks)
    ]
    loads += [
        pltpu.make_async_copy(operands[1 + k], ref, load_sems.at[k])
        for k, ref in enumerate((weights, owners, slots, lists))
    ]
    for load in loads:
        load.start()

    face, tile = lax.axis_index("face"), lax.axis_index("tile")
    n_face, n_tile = lax.axis_size("face"), lax.axis_size("tile")
    south = (lax.rem(face + 1, n_face), tile)
    north = (lax.rem(face + n_face - 1, n_face), tile)
    east = (face, lax.rem(tile + 1, n_tile))
    west = (face, lax.rem(tile + n_tile - 1, n_tile))
    toward = (south, north, east, west)

    barrier = pltpu.get_barrier_semaphore()
    for device in toward:
        pl.semaphore_signal(barrier, inc=1, device_id=device, device_id_type=MESH)
    pl.semaphore_wait(barrier, 4)
    for load in loads:
        load.wait()

    def store(c):
        return pltpu.make_async_copy(
            fields.at[steps, c],
            out.at[:, :, pl.ds(pl.multiple_of(c * width, width), width)],
            load_sems.at[4 + chunks + c],
        )

    def list_copy(s, c, j):
        return pltpu.make_async_remote_copy(
            src_ref=sending.at[s, c, j],
            dst_ref=received.at[s, c, j],
            send_sem=list_send.at[s, c, j],
            recv_sem=list_recv.at[s, c, j],
            device_id=toward[j],
            device_id_type=MESH,
        )

    def edge_copy(s, c, j):
        store, land, send, recv = (
            (tile_out, tile_in, tile_send, tile_recv)
            if j >= 2
            else (face_out, face_in, face_send, face_recv)
        )
        return pltpu.make_async_remote_copy(
            src_ref=store.at[s, c, j % 2],
            dst_ref=land.at[s, c, j % 2],
            send_sem=send.at[s, c, j % 2],
            recv_sem=recv.at[s, c, j % 2],
            device_id=toward[j],
            device_id_type=MESH,
        )

    def send_lists(s, c):
        for j in range(4):
            def pick(k, carry, j=j):
                elem = lists[s, 4 * face + j, tile * cap + k]
                sending[s, c, j, k] = fields[s, c, elem]
                return carry
            lax.fori_loop(0, cap, pick, 0, unroll=True)
            list_copy(s, c, j).start()

    def send_first(c, carry):
        send_lists(0, c)
        return carry

    ahead = min(AHEAD, chunks)
    lax.fori_loop(0, ahead, send_first, 0)

    lane = lax.broadcasted_iota(jnp.int32, (NODES, rows), 1)
    spread = jnp.where(
        (lane & (NODES - 1)) == lax.broadcasted_iota(jnp.int32, (NODES, rows), 0), 1.0, 0.0
    ).astype(jnp.float32)
    same = (lax.broadcasted_iota(jnp.int32, (rows, rows), 0) // NODES) == (
        lax.broadcasted_iota(jnp.int32, (rows, rows), 1) // NODES
    )
    def build(s, carry):
        repeated = jnp.dot(
            weights[s], spread, precision=HIGHEST, preferred_element_type=jnp.float32
        )
        high, low = halves(jnp.where(same, repeated, 0.0))
        mixing[s] = jnp.concatenate([high, low, high], axis=1)
        return carry

    lax.fori_loop(0, steps, build, 0)

    node = lax.broadcasted_iota(jnp.int32, (NODES, width), 0)
    flat_node = lax.broadcasted_iota(jnp.int32, (rows, width), 0) & (NODES - 1)

    def shift(block, amount):
        amount = amount % block.shape[0]
        return pltpu.roll(block, amount, 0) if amount else block

    def grid_of(flat):
        return flat.reshape(side, side, NODES, width)

    def pack(blocks, shifts, place):
        packed = shift(blocks[0], shifts[0])
        for k in range(1, side):
            packed = jnp.where(place == k, shift(blocks[k], shifts[k]), packed)
        return packed

    def interpolate(s, c):
        for j in range(4):
            list_copy(s, c, j).wait_recv()

        @pl.when((s == 0) & (c + ahead < chunks))
        def _():
            send_lists(0, c + ahead)

        arrived[...] = received[s, c]

        def pick(elem, carry):
            owner = owners[s, elem // side, elem % side]
            slot = slots[s, elem // side, elem % side]
            own = fields[s, c, slot]
            other = arrived[jnp.maximum(owner - 1, 0), jnp.minimum(slot, cap - 1)]
            source[elem] = jnp.where(owner == 0, own, other)
            return carry

        lax.fori_loop(0, elems, pick, 0, unroll=True)
        blocks = source[...]
        high, low = halves(blocks.reshape(rows, width))
        mixed = jnp.dot(
            mixing[s],
            jnp.concatenate([high, high, low], axis=0),
            preferred_element_type=jnp.float32,
        ).reshape(elems, NODES, width)
        mixed = jnp.clip(
            mixed, jnp.min(blocks, axis=1, keepdims=True), jnp.max(blocks, axis=1, keepdims=True)
        )
        grid = mixed.reshape(side, side, NODES, width)
        left = jnp.stack([shift(grid[x, 0], 3) for x in range(side)])[:, None]
        right = jnp.stack([shift(grid[x, side - 1], -3) for x in range(side)])[:, None]
        before = jnp.concatenate([left, grid[:, : side - 1]], axis=1).reshape(rows, width)
        after = jnp.concatenate([grid[:, 1:], right], axis=1).reshape(rows, width)
        flat = mixed.reshape(rows, width)
        flat = average(flat, before, after, (flat_node & 3) == 0, (flat_node & 3) == 3, 3)
        grid = grid_of(flat)
        above = jnp.stack([shift(grid[0, y], 12) for y in range(side)])[None]
        below = jnp.stack([shift(grid[side - 1, y], -12) for y in range(side)])[None]
        before = jnp.concatenate([above, grid[: side - 1]], axis=0).reshape(rows, width)
        after = jnp.concatenate([grid[1:], below], axis=0).reshape(rows, width)
        flat = average(flat, before, after, flat_node < 4, flat_node >= 12, 12)
        grid = grid_of(flat)
        fields[s + 1, c] = flat.reshape(elems, NODES, width)
        place = node & 3
        tile_out[s, c, 0] = pack(
            [grid[x, side - 1] for x in range(side)], [x - 3 for x in range(side)], place
        )
        tile_out[s, c, 1] = pack([grid[x, 0] for x in range(side)], list(range(side)), place)
        edge_copy(s, c, 2).start()
        edge_copy(s, c, 3).start()

    def average(flat, before, after, low, high, hop):
        return jnp.where(
            low,
            0.5 * (flat + shift(before, -hop)),
            jnp.where(high, 0.5 * (flat + shift(after, hop)), flat),
        )

    def blend(s, c, elem, beside, where):
        block = fields[s + 1, c, elem]
        fields[s + 1, c, elem] = jnp.where(where, 0.5 * (block + beside), block)

    def average_columns(s, c):
        edge_copy(s, c, 2).wait_recv()
        edge_copy(s, c, 3).wait_recv()
        from_west, from_east = tile_in[s, c, 0], tile_in[s, c, 1]
        for x in range(side):
            blend(s, c, x * side, shift(from_west, -x), (node & 3) == 0)
            blend(s, c, x * side + side - 1, shift(from_east, 3 - x), (node & 3) == 3)
        place = node >> 2
        face_out[s, c, 0] = pack(
            [fields[s + 1, c, (side - 1) * side + y] for y in range(side)],
            [4 * y - 12 for y in range(side)], place
        )
        face_out[s, c, 1] = pack(
            [fields[s + 1, c, y] for y in range(side)], [4 * y for y in range(side)], place
        )
        edge_copy(s, c, 0).start()
        edge_copy(s, c, 1).start()

    def average_rows(s, c):
        edge_copy(s, c, 0).wait_recv()
        edge_copy(s, c, 1).wait_recv()
        from_north, from_south = face_in[s, c, 0], face_in[s, c, 1]
        for y in range(side):
            blend(s, c, y, shift(from_north, -4 * y), node < 4)
            blend(s, c, (side - 1) * side + y, shift(from_south, 12 - 4 * y), node >= 12)

        @pl.when(s < steps - 1)
        def _():
            send_lists(s + 1, c)

        @pl.when(s == steps - 1)
        def _():
            store(c).start()

    phases = (interpolate, average_columns, average_rows)
    def advance(turn, carry):
        def advance_step(s, carry):
            for phase in (2, 1, 0):
                c = turn - chunks * (3 * s + phase)

                @pl.when((c >= 0) & (c < chunks))
                def _():
                    phases[phase](s, c)

            return carry

        return lax.fori_loop(0, steps, advance_step, carry)

    lax.fori_loop(0, chunks + chunks * (3 * steps - 1), advance, 0)

    def finish(k, carry):
        s, c = k // chunks, k % chunks
        for j in range(4):
            list_copy(s, c, j).wait_send()
            edge_copy(s, c, j).wait_send()
        return carry

    lax.fori_loop(0, steps * chunks, finish, 0)

    def finish_store(c, carry):
        store(c).wait()
        return carry

    lax.fori_loop(0, chunks, finish_store, 0)


def local(tracers, basis_weights, up_owner, up_slot, send_list):
    side = tracers.shape[0]
    columns = tracers.shape[3]
    steps = basis_weights.shape[0]
    elems = side * side
    rows = elems * NODES
    cap = send_list.shape[2] // lax.axis_size("tile")
    width = chunk_width(columns)
    chunks = columns // width
    dims = (steps, side, cap, chunks, width)
    whole = pl.BlockSpec(memory_space=pltpu.HBM)
    f32 = jnp.float32
    edges = pltpu.VMEM((steps, chunks, 2, NODES, width), f32)
    list_sems = pltpu.SemaphoreType.DMA((steps, chunks, 4))
    edge_sems = pltpu.SemaphoreType.DMA((steps, chunks, 2))
    result = pl.pallas_call(
        functools.partial(kernel, dims),
        out_shape=jax.ShapeDtypeStruct((elems, NODES, columns), f32),
        in_specs=[whole] * 5,
        out_specs=whole,
        scratch_shapes=[
            pltpu.VMEM((steps + 1, chunks, elems, NODES, width), f32),
            pltpu.VMEM((steps, rows, NODES), f32),
            pltpu.SMEM(up_owner.shape, jnp.int32),
            pltpu.SMEM(up_slot.shape, jnp.int32),
            pltpu.SMEM(send_list.shape, jnp.int32),
            pltpu.SemaphoreType.DMA((4 + 2 * chunks,)),
            pltpu.VMEM((steps, chunks, 4, cap, NODES, width), f32),
            pltpu.VMEM((4, cap, NODES, width), f32),
            pltpu.VMEM((steps, chunks, 4, cap, NODES, width), f32),
            pltpu.VMEM((steps, rows, 3 * rows), jnp.bfloat16),
            pltpu.VMEM((elems, NODES, width), f32),
            edges,
            edges,
            edges,
            edges,
            list_sems,
            list_sems,
            edge_sems,
            edge_sems,
            edge_sems,
            edge_sems,
        ],
        compiler_params=pltpu.CompilerParams(
            collective_id=0, has_side_effects=True, vmem_limit_bytes=62 * 1024 * 1024
        ),
        cost_estimate=pl.CostEstimate(
            flops=2 * steps * rows * NODES * columns,
            bytes_accessed=8 * rows * columns,
            transcendentals=0,
        ),
    )(
        tracers.reshape(elems, NODES, columns),
        basis_weights.reshape(steps, rows, NODES),
        up_owner,
        up_slot,
        send_list,
    )
    return result.reshape(side, side, NODES, columns)


def solution(mesh):
    return jax.shard_map(
        local,
        mesh=mesh,
        in_specs=(
            P("face", "tile", None, None),
            P(None, "face", "tile", None, None),
            P(None, "face", "tile"),
            P(None, "face", "tile"),
            P(),
        ),
        out_specs=P("face", "tile", None, None),
        check_vma=False,
    )
```

```python
import functools

import jax
import jax.numpy as jnp
from jax import lax
from jax.experimental import pallas as pl
from jax.experimental.pallas import tpu as pltpu
from jax.sharding import PartitionSpec as P

MESH = pl.DeviceIdType.MESH
NODES = 16
SLACK = 3
AHEAD = 3
HIGHEST = lax.Precision.HIGHEST


def chunk_width(columns):
    for width in (256, 128):
        if columns % width == 0:
            return width
    return columns


def halves(values):
    high = values.astype(jnp.bfloat16)
    return high, (values - high.astype(jnp.float32)).astype(jnp.bfloat16)


def kernel(dims, *refs):
    steps, side, cap, chunks, width = dims
    elems = side * side
    rows = elems * NODES
    operands, out, scratch = refs[:5], refs[5], refs[6:]
    (fields, weights, owners, slots, lists, load_sems, received, arrived, sending, mixing,
     source, tile_out, tile_in, face_out, face_in,
     list_send, list_recv, tile_send, tile_recv, face_send, face_recv) = scratch
    loads = [
        pltpu.make_async_copy(
            operands[0].at[:, :, pl.ds(c * width, width)], fields.at[0, c], load_sems.at[4 + c]
        )
        for c in range(chunks)
    ]
    loads += [
        pltpu.make_async_copy(operands[1 + k], ref, load_sems.at[k])
        for k, ref in enumerate((weights, owners, slots, lists))
    ]
    for load in loads:
        load.start()

    face, tile = lax.axis_index("face"), lax.axis_index("tile")
    n_face, n_tile = lax.axis_size("face"), lax.axis_size("tile")
    south = (lax.rem(face + 1, n_face), tile)
    north = (lax.rem(face + n_face - 1, n_face), tile)
    east = (face, lax.rem(tile + 1, n_tile))
    west = (face, lax.rem(tile + n_tile - 1, n_tile))
    toward = (south, north, east, west)

    barrier = pltpu.get_barrier_semaphore()
    for device in toward:
        pl.semaphore_signal(barrier, inc=1, device_id=device, device_id_type=MESH)
    pl.semaphore_wait(barrier, 4)
    for load in loads:
        load.wait()

    def store(c):
        return pltpu.make_async_copy(
            fields.at[steps, c],
            out.at[:, :, pl.ds(pl.multiple_of(c * width, width), width)],
            load_sems.at[4 + chunks + c],
        )

    def list_copy(s, c, j):
        return pltpu.make_async_remote_copy(
            src_ref=sending.at[s, c, j],
            dst_ref=received.at[s, c, j],
            send_sem=list_send.at[s, c, j],
            recv_sem=list_recv.at[s, c, j],
            device_id=toward[j],
            device_id_type=MESH,
        )

    def edge_copy(s, c, j):
        store, land, send, recv = (
            (tile_out, tile_in, tile_send, tile_recv)
            if j >= 2
            else (face_out, face_in, face_send, face_recv)
        )
        return pltpu.make_async_remote_copy(
            src_ref=store.at[s, c, j % 2],
            dst_ref=land.at[s, c, j % 2],
            send_sem=send.at[s, c, j % 2],
            recv_sem=recv.at[s, c, j % 2],
            device_id=toward[j],
            device_id_type=MESH,
        )

    def send_lists(s, c):
        for j in range(4):
            def pick(k, carry, j=j):
                elem = lists[s, 4 * face + j, tile * cap + k]
                sending[s, c, j, k] = fields[s, c, elem]
                return carry
            lax.fori_loop(0, cap, pick, 0, unroll=True)
            list_copy(s, c, j).start()

    def send_first(c, carry):
        send_lists(0, c)
        return carry

    ahead = min(AHEAD, chunks)
    lax.fori_loop(0, ahead, send_first, 0)

    lane = lax.broadcasted_iota(jnp.int32, (NODES, rows), 1)
    spread = jnp.where(
        (lane & (NODES - 1)) == lax.broadcasted_iota(jnp.int32, (NODES, rows), 0), 1.0, 0.0
    ).astype(jnp.float32)
    same = (lax.broadcasted_iota(jnp.int32, (rows, rows), 0) // NODES) == (
        lax.broadcasted_iota(jnp.int32, (rows, rows), 1) // NODES
    )
    def build(s, carry):
        repeated = jnp.dot(
            weights[s], spread, precision=HIGHEST, preferred_element_type=jnp.float32
        )
        high, low = halves(jnp.where(same, repeated, 0.0))
        mixing[s] = jnp.concatenate([high, low, high], axis=1)
        return carry

    lax.fori_loop(0, steps, build, 0)

    node = lax.broadcasted_iota(jnp.int32, (NODES, width), 0)
    flat_node = lax.broadcasted_iota(jnp.int32, (rows, width), 0) & (NODES - 1)

    def shift(block, amount):
        amount = amount % block.shape[0]
        return pltpu.roll(block, amount, 0) if amount else block

    def grid_of(flat):
        return flat.reshape(side, side, NODES, width)

    def pack(blocks, shifts, place):
        packed = shift(blocks[0], shifts[0])
        for k in range(1, side):
            packed = jnp.where(place == k, shift(blocks[k], shifts[k]), packed)
        return packed

    def interpolate(s, c):
        for j in range(4):
            list_copy(s, c, j).wait_recv()

        @pl.when((s == 0) & (c + ahead < chunks))
        def _():
            send_lists(0, c + ahead)

        arrived[...] = received[s, c]

        def pick(elem, carry):
            owner = owners[s, elem // side, elem % side]
            slot = slots[s, elem // side, elem % side]
            own = fields[s, c, slot]
            other = arrived[jnp.maximum(owner - 1, 0), jnp.minimum(slot, cap - 1)]
            source[elem] = jnp.where(owner == 0, own, other)
            return carry

        lax.fori_loop(0, elems, pick, 0, unroll=True)
        blocks = source[...]
        high, low = halves(blocks.reshape(rows, width))
        mixed = jnp.dot(
            mixing[s],
            jnp.concatenate([high, high, low], axis=0),
            preferred_element_type=jnp.float32,
        ).reshape(elems, NODES, width)
        mixed = jnp.clip(
            mixed, jnp.min(blocks, axis=1, keepdims=True), jnp.max(blocks, axis=1, keepdims=True)
        )
        grid = mixed.reshape(side, side, NODES, width)
        left = jnp.stack([shift(grid[x, 0], 3) for x in range(side)])[:, None]
        right = jnp.stack([shift(grid[x, side - 1], -3) for x in range(side)])[:, None]
        before = jnp.concatenate([left, grid[:, : side - 1]], axis=1).reshape(rows, width)
        after = jnp.concatenate([grid[:, 1:], right], axis=1).reshape(rows, width)
        flat = mixed.reshape(rows, width)
        flat = average(flat, before, after, (flat_node & 3) == 0, (flat_node & 3) == 3, 3)
        grid = grid_of(flat)
        above = jnp.stack([shift(grid[0, y], 12) for y in range(side)])[None]
        below = jnp.stack([shift(grid[side - 1, y], -12) for y in range(side)])[None]
        before = jnp.concatenate([above, grid[: side - 1]], axis=0).reshape(rows, width)
        after = jnp.concatenate([grid[1:], below], axis=0).reshape(rows, width)
        flat = average(flat, before, after, flat_node < 4, flat_node >= 12, 12)
        grid = grid_of(flat)
        fields[s + 1, c] = flat.reshape(elems, NODES, width)
        place = node & 3
        tile_out[s, c, 0] = pack(
            [grid[x, side - 1] for x in range(side)], [x - 3 for x in range(side)], place
        )
        tile_out[s, c, 1] = pack([grid[x, 0] for x in range(side)], list(range(side)), place)
        edge_copy(s, c, 2).start()
        edge_copy(s, c, 3).start()

    def average(flat, before, after, low, high, hop):
        return jnp.where(
            low,
            0.5 * (flat + shift(before, -hop)),
            jnp.where(high, 0.5 * (flat + shift(after, hop)), flat),
        )

    def blend(s, c, elem, beside, where):
        block = fields[s + 1, c, elem]
        fields[s + 1, c, elem] = jnp.where(where, 0.5 * (block + beside), block)

    def average_columns(s, c):
        edge_copy(s, c, 2).wait_recv()
        edge_copy(s, c, 3).wait_recv()
        from_west, from_east = tile_in[s, c, 0], tile_in[s, c, 1]
        for x in range(side):
            blend(s, c, x * side, shift(from_west, -x), (node & 3) == 0)
            blend(s, c, x * side + side - 1, shift(from_east, 3 - x), (node & 3) == 3)
        place = node >> 2
        face_out[s, c, 0] = pack(
            [fields[s + 1, c, (side - 1) * side + y] for y in range(side)],
            [4 * y - 12 for y in range(side)], place
        )
        face_out[s, c, 1] = pack(
            [fields[s + 1, c, y] for y in range(side)], [4 * y for y in range(side)], place
        )
        edge_copy(s, c, 0).start()
        edge_copy(s, c, 1).start()

    def average_rows(s, c):
        edge_copy(s, c, 0).wait_recv()
        edge_copy(s, c, 1).wait_recv()
        from_north, from_south = face_in[s, c, 0], face_in[s, c, 1]
        for y in range(side):
            blend(s, c, y, shift(from_north, -4 * y), node < 4)
            blend(s, c, (side - 1) * side + y, shift(from_south, 12 - 4 * y), node >= 12)

        @pl.when(s < steps - 1)
        def _():
            send_lists(s + 1, c)

        @pl.when(s == steps - 1)
        def _():
            store(c).start()

    phases = (interpolate, average_columns, average_rows)
    def advance(turn, carry):
        def advance_step(s, carry):
            for phase in (2, 1, 0):
                c = turn - SLACK * (3 * s + phase)

                @pl.when((c >= 0) & (c < chunks))
                def _():
                    phases[phase](s, c)

            return carry

        return lax.fori_loop(0, steps, advance_step, carry)

    lax.fori_loop(0, chunks + SLACK * (3 * steps - 1), advance, 0)

    def finish(k, carry):
        s, c = k // chunks, k % chunks
        for j in range(4):
            list_copy(s, c, j).wait_send()
            edge_copy(s, c, j).wait_send()
        return carry

    lax.fori_loop(0, steps * chunks, finish, 0)

    def finish_store(c, carry):
        store(c).wait()
        return carry

    lax.fori_loop(0, chunks, finish_store, 0)


def local(tracers, basis_weights, up_owner, up_slot, send_list):
    side = tracers.shape[0]
    columns = tracers.shape[3]
    steps = basis_weights.shape[0]
    elems = side * side
    rows = elems * NODES
    cap = send_list.shape[2] // lax.axis_size("tile")
    width = chunk_width(columns)
    chunks = columns // width
    dims = (steps, side, cap, chunks, width)
    whole = pl.BlockSpec(memory_space=pltpu.HBM)
    f32 = jnp.float32
    edges = pltpu.VMEM((steps, chunks, 2, NODES, width), f32)
    list_sems = pltpu.SemaphoreType.DMA((steps, chunks, 4))
    edge_sems = pltpu.SemaphoreType.DMA((steps, chunks, 2))
    result = pl.pallas_call(
        functools.partial(kernel, dims),
        out_shape=jax.ShapeDtypeStruct((elems, NODES, columns), f32),
        in_specs=[whole] * 5,
        out_specs=whole,
        scratch_shapes=[
            pltpu.VMEM((steps + 1, chunks, elems, NODES, width), f32),
            pltpu.VMEM((steps, rows, NODES), f32),
            pltpu.SMEM(up_owner.shape, jnp.int32),
            pltpu.SMEM(up_slot.shape, jnp.int32),
            pltpu.SMEM(send_list.shape, jnp.int32),
            pltpu.SemaphoreType.DMA((4 + 2 * chunks,)),
            pltpu.VMEM((steps, chunks, 4, cap, NODES, width), f32),
            pltpu.VMEM((4, cap, NODES, width), f32),
            pltpu.VMEM((steps, chunks, 4, cap, NODES, width), f32),
            pltpu.VMEM((steps, rows, 3 * rows), jnp.bfloat16),
            pltpu.VMEM((elems, NODES, width), f32),
            edges,
            edges,
            edges,
            edges,
            list_sems,
            list_sems,
            edge_sems,
            edge_sems,
            edge_sems,
            edge_sems,
        ],
        compiler_params=pltpu.CompilerParams(
            collective_id=0, has_side_effects=True, vmem_limit_bytes=62 * 1024 * 1024
        ),
        cost_estimate=pl.CostEstimate(
            flops=2 * steps * rows * NODES * columns,
            bytes_accessed=8 * rows * columns,
            transcendentals=0,
        ),
    )(
        tracers.reshape(elems, NODES, columns),
        basis_weights.reshape(steps, rows, NODES),
        up_owner,
        up_slot,
        send_list,
    )
    return result.reshape(side, side, NODES, columns)


def solution(mesh):
    return jax.shard_map(
        local,
        mesh=mesh,
        in_specs=(
            P("face", "tile", None, None),
            P(None, "face", "tile", None, None),
            P(None, "face", "tile"),
            P(None, "face", "tile"),
            P(),
        ),
        out_specs=P("face", "tile", None, None),
        check_vma=False,
    )
```

```python
import functools

import jax
import jax.numpy as jnp
from jax import lax
from jax.experimental import pallas as pl
from jax.experimental.pallas import tpu as pltpu
from jax.sharding import PartitionSpec as P

MESH = pl.DeviceIdType.MESH
NODES = 16
SLACK = 3
AHEAD = 5
HIGHEST = lax.Precision.HIGHEST


def chunk_width(columns):
    for width in (256, 128):
        if columns % width == 0:
            return width
    return columns


def halves(values):
    high = values.astype(jnp.bfloat16)
    return high, (values - high.astype(jnp.float32)).astype(jnp.bfloat16)


def kernel(dims, *refs):
    steps, side, cap, chunks, width = dims
    elems = side * side
    rows = elems * NODES
    operands, out, scratch = refs[:5], refs[5], refs[6:]
    (fields, weights, owners, slots, lists, load_sems, received, arrived, sending, mixing,
     source, tile_out, tile_in, face_out, face_in,
     list_send, list_recv, tile_send, tile_recv, face_send, face_recv) = scratch
    loads = [
        pltpu.make_async_copy(
            operands[0].at[:, :, pl.ds(c * width, width)], fields.at[0, c], load_sems.at[4 + c]
        )
        for c in range(chunks)
    ]
    loads += [
        pltpu.make_async_copy(operands[1 + k], ref, load_sems.at[k])
        for k, ref in enumerate((weights, owners, slots, lists))
    ]
    for load in loads:
        load.start()

    face, tile = lax.axis_index("face"), lax.axis_index("tile")
    n_face, n_tile = lax.axis_size("face"), lax.axis_size("tile")
    south = (lax.rem(face + 1, n_face), tile)
    north = (lax.rem(face + n_face - 1, n_face), tile)
    east = (face, lax.rem(tile + 1, n_tile))
    west = (face, lax.rem(tile + n_tile - 1, n_tile))
    toward = (south, north, east, west)

    barrier = pltpu.get_barrier_semaphore()
    for device in toward:
        pl.semaphore_signal(barrier, inc=1, device_id=device, device_id_type=MESH)
    pl.semaphore_wait(barrier, 4)
    for load in loads:
        load.wait()

    def store(c):
        return pltpu.make_async_copy(
            fields.at[steps, c],
            out.at[:, :, pl.ds(pl.multiple_of(c * width, width), width)],
            load_sems.at[4 + chunks + c],
        )

    def list_copy(s, c, j):
        return pltpu.make_async_remote_copy(
            src_ref=sending.at[s, c, j],
            dst_ref=received.at[s, c, j],
            send_sem=list_send.at[s, c, j],
            recv_sem=list_recv.at[s, c, j],
            device_id=toward[j],
            device_id_type=MESH,
        )

    def edge_copy(s, c, j):
        store, land, send, recv = (
            (tile_out, tile_in, tile_send, tile_recv)
            if j >= 2
            else (face_out, face_in, face_send, face_recv)
        )
        return pltpu.make_async_remote_copy(
            src_ref=store.at[s, c, j % 2],
            dst_ref=land.at[s, c, j % 2],
            send_sem=send.at[s, c, j % 2],
            recv_sem=recv.at[s, c, j % 2],
            device_id=toward[j],
            device_id_type=MESH,
        )

    def send_lists(s, c):
        for j in range(4):
            def pick(k, carry, j=j):
                elem = lists[s, 4 * face + j, tile * cap + k]
                sending[s, c, j, k] = fields[s, c, elem]
                return carry
            lax.fori_loop(0, cap, pick, 0, unroll=True)
            list_copy(s, c, j).start()

    def send_first(c, carry):
        send_lists(0, c)
        return carry

    ahead = min(AHEAD, chunks)
    lax.fori_loop(0, ahead, send_first, 0)

    lane = lax.broadcasted_iota(jnp.int32, (NODES, rows), 1)
    spread = jnp.where(
        (lane & (NODES - 1)) == lax.broadcasted_iota(jnp.int32, (NODES, rows), 0), 1.0, 0.0
    ).astype(jnp.float32)
    same = (lax.broadcasted_iota(jnp.int32, (rows, rows), 0) // NODES) == (
        lax.broadcasted_iota(jnp.int32, (rows, rows), 1) // NODES
    )
    def build(s, carry):
        repeated = jnp.dot(
            weights[s], spread, precision=HIGHEST, preferred_element_type=jnp.float32
        )
        high, low = halves(jnp.where(same, repeated, 0.0))
        mixing[s] = jnp.concatenate([high, low, high], axis=1)
        return carry

    lax.fori_loop(0, steps, build, 0)

    node = lax.broadcasted_iota(jnp.int32, (NODES, width), 0)
    flat_node = lax.broadcasted_iota(jnp.int32, (rows, width), 0) & (NODES - 1)

    def shift(block, amount):
        amount = amount % block.shape[0]
        return pltpu.roll(block, amount, 0) if amount else block

    def grid_of(flat):
        return flat.reshape(side, side, NODES, width)

    def pack(blocks, shifts, place):
        packed = shift(blocks[0], shifts[0])
        for k in range(1, side):
            packed = jnp.where(place == k, shift(blocks[k], shifts[k]), packed)
        return packed

    def interpolate(s, c):
        for j in range(4):
            list_copy(s, c, j).wait_recv()

        @pl.when((s == 0) & (c + ahead < chunks))
        def _():
            send_lists(0, c + ahead)

        arrived[...] = received[s, c]

        def pick(elem, carry):
            owner = owners[s, elem // side, elem % side]
            slot = slots[s, elem // side, elem % side]
            own = fields[s, c, slot]
            other = arrived[jnp.maximum(owner - 1, 0), jnp.minimum(slot, cap - 1)]
            source[elem] = jnp.where(owner == 0, own, other)
            return carry

        lax.fori_loop(0, elems, pick, 0, unroll=True)
        blocks = source[...]
        high, low = halves(blocks.reshape(rows, width))
        mixed = jnp.dot(
            mixing[s],
            jnp.concatenate([high, high, low], axis=0),
            preferred_element_type=jnp.float32,
        ).reshape(elems, NODES, width)
        mixed = jnp.clip(
            mixed, jnp.min(blocks, axis=1, keepdims=True), jnp.max(blocks, axis=1, keepdims=True)
        )
        grid = mixed.reshape(side, side, NODES, width)
        left = jnp.stack([shift(grid[x, 0], 3) for x in range(side)])[:, None]
        right = jnp.stack([shift(grid[x, side - 1], -3) for x in range(side)])[:, None]
        before = jnp.concatenate([left, grid[:, : side - 1]], axis=1).reshape(rows, width)
        after = jnp.concatenate([grid[:, 1:], right], axis=1).reshape(rows, width)
        flat = mixed.reshape(rows, width)
        flat = average(flat, before, after, (flat_node & 3) == 0, (flat_node & 3) == 3, 3)
        grid = grid_of(flat)
        above = jnp.stack([shift(grid[0, y], 12) for y in range(side)])[None]
        below = jnp.stack([shift(grid[side - 1, y], -12) for y in range(side)])[None]
        before = jnp.concatenate([above, grid[: side - 1]], axis=0).reshape(rows, width)
        after = jnp.concatenate([grid[1:], below], axis=0).reshape(rows, width)
        flat = average(flat, before, after, flat_node < 4, flat_node >= 12, 12)
        grid = grid_of(flat)
        fields[s + 1, c] = flat.reshape(elems, NODES, width)
        place = node & 3
        tile_out[s, c, 0] = pack(
            [grid[x, side - 1] for x in range(side)], [x - 3 for x in range(side)], place
        )
        tile_out[s, c, 1] = pack([grid[x, 0] for x in range(side)], list(range(side)), place)
        edge_copy(s, c, 2).start()
        edge_copy(s, c, 3).start()

    def average(flat, before, after, low, high, hop):
        return jnp.where(
            low,
            0.5 * (flat + shift(before, -hop)),
            jnp.where(high, 0.5 * (flat + shift(after, hop)), flat),
        )

    def blend(s, c, elem, beside, where):
        block = fields[s + 1, c, elem]
        fields[s + 1, c, elem] = jnp.where(where, 0.5 * (block + beside), block)

    def average_columns(s, c):
        edge_copy(s, c, 2).wait_recv()
        edge_copy(s, c, 3).wait_recv()
        from_west, from_east = tile_in[s, c, 0], tile_in[s, c, 1]
        for x in range(side):
            blend(s, c, x * side, shift(from_west, -x), (node & 3) == 0)
            blend(s, c, x * side + side - 1, shift(from_east, 3 - x), (node & 3) == 3)
        place = node >> 2
        face_out[s, c, 0] = pack(
            [fields[s + 1, c, (side - 1) * side + y] for y in range(side)],
            [4 * y - 12 for y in range(side)], place
        )
        face_out[s, c, 1] = pack(
            [fields[s + 1, c, y] for y in range(side)], [4 * y for y in range(side)], place
        )
        edge_copy(s, c, 0).start()
        edge_copy(s, c, 1).start()

    def average_rows(s, c):
        edge_copy(s, c, 0).wait_recv()
        edge_copy(s, c, 1).wait_recv()
        from_north, from_south = face_in[s, c, 0], face_in[s, c, 1]
        for y in range(side):
            blend(s, c, y, shift(from_north, -4 * y), node < 4)
            blend(s, c, (side - 1) * side + y, shift(from_south, 12 - 4 * y), node >= 12)

        @pl.when(s < steps - 1)
        def _():
            send_lists(s + 1, c)

        @pl.when(s == steps - 1)
        def _():
            store(c).start()

    phases = (interpolate, average_columns, average_rows)
    def advance(turn, carry):
        def advance_step(s, carry):
            for phase in (2, 1, 0):
                c = turn - SLACK * (3 * s + phase)

                @pl.when((c >= 0) & (c < chunks))
                def _():
                    phases[phase](s, c)

            return carry

        return lax.fori_loop(0, steps, advance_step, carry)

    lax.fori_loop(0, chunks + SLACK * (3 * steps - 1), advance, 0)

    def finish(k, carry):
        s, c = k // chunks, k % chunks
        for j in range(4):
            list_copy(s, c, j).wait_send()
            edge_copy(s, c, j).wait_send()
        return carry

    lax.fori_loop(0, steps * chunks, finish, 0)

    def finish_store(c, carry):
        store(c).wait()
        return carry

    lax.fori_loop(0, chunks, finish_store, 0)


def local(tracers, basis_weights, up_owner, up_slot, send_list):
    side = tracers.shape[0]
    columns = tracers.shape[3]
    steps = basis_weights.shape[0]
    elems = side * side
    rows = elems * NODES
    cap = send_list.shape[2] // lax.axis_size("tile")
    width = chunk_width(columns)
    chunks = columns // width
    dims = (steps, side, cap, chunks, width)
    whole = pl.BlockSpec(memory_space=pltpu.HBM)
    f32 = jnp.float32
    edges = pltpu.VMEM((steps, chunks, 2, NODES, width), f32)
    list_sems = pltpu.SemaphoreType.DMA((steps, chunks, 4))
    edge_sems = pltpu.SemaphoreType.DMA((steps, chunks, 2))
    result = pl.pallas_call(
        functools.partial(kernel, dims),
        out_shape=jax.ShapeDtypeStruct((elems, NODES, columns), f32),
        in_specs=[whole] * 5,
        out_specs=whole,
        scratch_shapes=[
            pltpu.VMEM((steps + 1, chunks, elems, NODES, width), f32),
            pltpu.VMEM((steps, rows, NODES), f32),
            pltpu.SMEM(up_owner.shape, jnp.int32),
            pltpu.SMEM(up_slot.shape, jnp.int32),
            pltpu.SMEM(send_list.shape, jnp.int32),
            pltpu.SemaphoreType.DMA((4 + 2 * chunks,)),
            pltpu.VMEM((steps, chunks, 4, cap, NODES, width), f32),
            pltpu.VMEM((4, cap, NODES, width), f32),
            pltpu.VMEM((steps, chunks, 4, cap, NODES, width), f32),
            pltpu.VMEM((steps, rows, 3 * rows), jnp.bfloat16),
            pltpu.VMEM((elems, NODES, width), f32),
            edges,
            edges,
            edges,
            edges,
            list_sems,
            list_sems,
            edge_sems,
            edge_sems,
            edge_sems,
            edge_sems,
        ],
        compiler_params=pltpu.CompilerParams(
            collective_id=0, has_side_effects=True, vmem_limit_bytes=62 * 1024 * 1024
        ),
        cost_estimate=pl.CostEstimate(
            flops=2 * steps * rows * NODES * columns,
            bytes_accessed=8 * rows * columns,
            transcendentals=0,
        ),
    )(
        tracers.reshape(elems, NODES, columns),
        basis_weights.reshape(steps, rows, NODES),
        up_owner,
        up_slot,
        send_list,
    )
    return result.reshape(side, side, NODES, columns)


def solution(mesh):
    return jax.shard_map(
        local,
        mesh=mesh,
        in_specs=(
            P("face", "tile", None, None),
            P(None, "face", "tile", None, None),
            P(None, "face", "tile"),
            P(None, "face", "tile"),
            P(),
        ),
        out_specs=P("face", "tile", None, None),
        check_vma=False,
    )
```
